32 devices in a mesh: dp: 4 (over x, core), ctx: 8 (over z, y).
Axes of the slice: x: 2, y: 2, z: 4, core: 2. Of those that a mesh axis runs over, the one named last changes fastest.
Arguments:
- queries: bfloat16 [4, 1024, 2048], P('dp', 'ctx'), may hold values from -6 to 6
- keys: bfloat16 [4, 1024, 2048], P('dp', 'ctx'), may hold values from -6 to 6
- values: bfloat16 [4, 1024, 2048], P('dp', 'ctx'), may hold values from -6 to 6
- out_grad: bfloat16 [4, 1024, 2048], P('dp', 'ctx'), may hold values from -6 to 6
- out_proj: bfloat16 [2048, 2048], P('dp'), may hold values from -0.125 to 0.125
- attn_out: bfloat16 [4, 1024, 2048], P('dp', 'ctx'), may hold values from -3 to 3
- log_sum: float32 [4, 16, 1024], P('dp', None, 'ctx'), may hold values from 3 to 5
- group_order: int32 [4, 32], P('dp'), may hold values from 0 to 31, each once within a row
Outputs:
- query_grad: bfloat16 [4, 1024, 2048], P('dp', 'ctx')
- key_grad: bfloat16 [4, 1024, 2048], P('dp', 'ctx')
- value_grad: bfloat16 [4, 1024, 2048], P('dp', 'ctx')
The draws below stay inside these ranges and needn't reach their ends.
Inputs may be any that keep to these rules, and one draw needn't show every extreme that they name: `group_order`: each row holds every number once.
All inputs are finite; a program needn't handle non-finite values.
Results may differ from the reference program's by a relative error of at most 0.0075.
Values may be sent and summed in bfloat16 or wider, within the bound.
No kernel may reach another device: no remote copies, remote signals or barrier semaphores. Data moves between devices by JAX's collectives and lax.ppermute only.
A program may use at most 64 MiB of HBM per device.

```python
import jax
import jax.numpy as jnp
from jax import lax

HEADS = 16
DH = 128
DW = 2048
GROUP = 32
TOK = 128
CPD = 4
BLOCKS = 8
GROUPS = 32
LEN = 1024
SEQS = 4


def steps_of(own_key, shape, pieces, least, high):
    loudness = 1.0
    for dim, blocks in pieces:
        draws = jax.random.uniform(jax.random.fold_in(jax.random.fold_in(own_key, 6), dim), (blocks,), jnp.float32, least / len(pieces), high / len(pieces))
        loudness = loudness * jnp.repeat(jnp.exp(draws), shape[dim] // blocks).reshape((-1,) + (1,) * (len(shape) - 1 - dim))
    return loudness


def bell_draw(key, shape, width, limit, pieces=(), kind=jnp.bfloat16):
    loudness = steps_of(key, shape, pieces, -0.22, 0.18) if pieces else 1.0
    values = jax.random.normal(key, shape, jnp.float32) * width * loudness
    return jnp.minimum(jnp.maximum(values, -limit), limit).astype(kind)


def setup_inputs(seed: int = 0) -> dict:
    splits = jax.random.split(jax.random.key(seed), 9)
    queries = bell_draw(splits[0], (SEQS, LEN, HEADS * DH), 1.0, 6.0, ((0, 4), (1, 8)))
    keys = bell_draw(splits[1], (SEQS, LEN, HEADS * DH), 1.0, 6.0, ((0, 4), (1, 8)))
    values = bell_draw(splits[2], (SEQS, LEN, HEADS * DH), 1.0, 6.0, ((0, 4), (1, 8)))
    out_grad = bell_draw(splits[3], (SEQS, LEN, DW), 1.0, 6.0, ((0, 4), (1, 8)))
    out_proj = bell_draw(splits[4], (DW, HEADS * DH), DW ** -0.5, 0.125, ((0, 4),))
    attn_out = bell_draw(splits[5], (SEQS, LEN, HEADS * DH), 0.5, 3.0, ((0, 4), (1, 8)))
    log_sum = jnp.clip(3.0 + 2.0 * jax.random.uniform(splits[6], (SEQS, HEADS, LEN), jnp.float32) ** steps_of(splits[6], (SEQS, HEADS, LEN), ((0, 4), (2, 8)), -0.2, 0.2), 3.0, 5.0)
    group_order = jax.vmap(lambda own: jax.random.permutation(own, GROUPS))(jax.random.split(splits[7], SEQS)).reshape((SEQS, GROUPS)).astype(jnp.int32)
    return dict(queries=queries, keys=keys, values=values, out_grad=out_grad, out_proj=out_proj, attn_out=attn_out, log_sum=log_sum, group_order=group_order)


def pair_grads(query_blk, grad_blk, lse_blk, delta_blk, query_pos, key_blk, value_blk, key_pos):
    factor = DH ** -0.5
    query_f = query_blk.astype(jnp.float32)
    grad_f = grad_blk.astype(jnp.float32)
    key_f = key_blk.astype(jnp.float32)
    value_f = value_blk.astype(jnp.float32)
    scores = jnp.einsum('nqhd,nkhd->nhqk', query_f, key_f) * factor
    visible = key_pos[:, None, None, :] <= query_pos[:, None, :, None]
    probs = jnp.where(visible, jnp.exp(scores - lse_blk[:, :, :, None]), 0.0)
    probs_low = lax.optimization_barrier(probs.astype(jnp.bfloat16)).astype(jnp.float32)
    value_part = jnp.einsum('nhqk,nqhd->nkhd', probs_low, grad_f)
    dprobs = jnp.einsum('nqhd,nkhd->nhqk', grad_f, value_f)
    dscores = (probs * (dprobs - delta_blk[:, :, :, None])).astype(jnp.bfloat16)
    dscores = lax.optimization_barrier(dscores).astype(jnp.float32)
    query_part = jnp.einsum('nhqk,nkhd->nqhd', dscores, key_f) * factor
    key_part = jnp.einsum('nhqk,nqhd->nkhd', dscores, query_f) * factor
    return query_part, key_part, value_part


def reference(queries, keys, values, out_grad, out_proj, attn_out, log_sum, group_order):
    def blocks(array):
        return array.reshape(BLOCKS, TOK, HEADS, DH)

    def one_sequence(items):
        query, key, value, upstream, output, lse, order = items
        attn_grad = jnp.dot(upstream, out_proj, preferred_element_type=jnp.float32).astype(jnp.bfloat16)
        grad_b = blocks(attn_grad)
        delta_b = jnp.sum(grad_b.astype(jnp.float32) * blocks(output).astype(jnp.float32), axis=3).transpose(0, 2, 1)
        lse_b = lse.reshape(HEADS, BLOCKS, TOK).transpose(1, 0, 2)
        offsets = jnp.arange(GROUP, dtype=jnp.int32)
        position = (order.reshape(BLOCKS, CPD)[:, :, None] * GROUP + offsets[None, None, :]).reshape(BLOCKS, TOK)
        query_b = blocks(query)
        key_b = blocks(key)
        value_b = blocks(value)
        own = pair_grads(query_b, grad_b, lse_b, delta_b, position, key_b, value_b, position)
        cross = pair_grads(query_b, grad_b, lse_b, delta_b, position,
                           jnp.roll(key_b, 1, axis=0), jnp.roll(value_b, 1, axis=0), jnp.roll(position, 1, axis=0))
        query_total = own[0] + cross[0]
        key_total = own[1] + jnp.roll(cross[1], -1, axis=0)
        value_total = own[2] + jnp.roll(cross[2], -1, axis=0)
        return (query_total.reshape(LEN, HEADS * DH).astype(jnp.bfloat16),
                key_total.reshape(LEN, HEADS * DH).astype(jnp.bfloat16),
                value_total.reshape(LEN, HEADS * DH).astype(jnp.bfloat16))

    results = lax.map(one_sequence, (queries, keys, values, out_grad, attn_out, log_sum, group_order))
    return (results[0], results[1], results[2])
```

```python
import functools

import jax
import jax.numpy as jnp
from jax import lax
from jax.experimental import pallas as pl
from jax.experimental.pallas import tpu as pltpu
from jax.sharding import PartitionSpec as P

GROUP = 32
CHUNKS = 2
LANES = 512
EXTRA = 16
F32 = jnp.float32
BF16 = jnp.bfloat16


def dot(a, b, ca, cb):
    return lax.dot_general(a, b, (((ca,), (cb,)), ((), ())), preferred_element_type=F32)


def vmem(shape=None, index=None):
    if shape is None:
        return pl.BlockSpec(memory_space=pltpu.VMEM)
    return pl.BlockSpec(shape, index)


def params():
    return pltpu.CompilerParams(vmem_limit_bytes=24 * 1024 * 1024)


def cost(flops, nbytes, exps=0):
    return pl.CostEstimate(flops=int(flops), bytes_accessed=int(nbytes), transcendentals=int(exps))


def project_kernel(chips, pair, *refs):
    lhs, weights = refs[:chips], refs[chips : chips + pair]
    local, remote = refs[chips + pair], refs[chips + pair + 1 :]
    rows = weights[0].shape[0]
    tokens = lhs[0].shape[0]
    stacked = jnp.concatenate([ref[...] for ref in lhs], axis=0)
    total = dot(stacked[:, :rows], weights[0][...], 1, 0)
    for i in range(1, pair):
        total += dot(stacked[:, i * rows : (i + 1) * rows], weights[i][...], 1, 0)
    local[...] = total[:tokens]
    for j, ref in enumerate(remote):
        ref[...] = total[(j + 1) * tokens : (j + 2) * tokens].astype(BF16)


def project(lhs, weights, first, width):
    chips, pair = len(lhs), len(weights)
    tokens, depth = lhs[0].shape
    rows = weights[0].shape[0]
    tile = min(LANES, width)
    base = first // tile
    return pl.pallas_call(
        functools.partial(project_kernel, chips, pair),
        grid=(width // tile,),
        in_specs=[vmem((tokens, depth), lambda i: (0, 0))] * chips
        + [vmem((rows, tile), lambda i: (0, base + i))] * pair,
        out_specs=[vmem((tokens, tile), lambda i: (0, i))] * chips,
        out_shape=[jax.ShapeDtypeStruct((tokens, width), F32)]
        + [jax.ShapeDtypeStruct((tokens, width), BF16)] * (chips - 1),
        compiler_params=params(),
        cost_estimate=cost(2 * chips * tokens * depth * width, 2 * depth * width),
        name="project",
    )(*lhs, *weights)


def grad_kernel(heads, local, *refs):
    parts, out_ref, msg = refs[:-2], refs[-2], refs[-1]
    tokens = local.shape[0]
    size = local.shape[1] // heads
    total = local[...]
    for ref in parts:
        total += ref[...].astype(F32)
    grad = total.astype(BF16)
    msg[:tokens, :] = grad
    product = grad.astype(F32) * out_ref[...].astype(F32)
    high = product.astype(BF16)
    low = (product - high.astype(F32)).astype(BF16)
    ones = jnp.ones((8, size), BF16)
    rows = []
    for h in range(heads):
        cols = slice(h * size, (h + 1) * size)
        rows.append(dot(ones, high[:, cols], 1, 1) + dot(ones, low[:, cols], 1, 1))
    delta = jnp.concatenate(rows, axis=1)
    top = delta.astype(BF16).astype(F32)
    pick = lax.broadcasted_iota(jnp.int32, delta.shape, 0)
    both = jnp.where(pick == 0, top, delta - top)
    msg[tokens:, :] = jnp.concatenate([both, both], axis=0).astype(BF16)


def combine(local, parts, attn_out, first, heads):
    tokens, width = local.shape
    return pl.pallas_call(
        functools.partial(grad_kernel, heads),
        grid=(1,),
        in_specs=[vmem((tokens, width), lambda i: (0, 0))] * (1 + len(parts))
        + [vmem((tokens, width), lambda i: (0, first // width))],
        out_specs=vmem((tokens + EXTRA, width), lambda i: (0, 0)),
        out_shape=jax.ShapeDtypeStruct((tokens + EXTRA, width), BF16),
        compiler_params=params(),
        cost_estimate=cost(tokens * width * 64, tokens * width * 10),
        name="combine",
    )(local, *parts, attn_out)


def delta_row(msg, tokens, cols):
    tail = msg[tokens:, cols].astype(F32)
    return tail[0:1] + tail[1:2]


def own_kernel(heads, head0, query, key, value, msg, lse, bias, dq, dk, dv):
    tokens = query.shape[0]
    size = query.shape[1] // heads
    factor = size ** -0.5
    mask = bias[...]
    for h in range(heads):
        cols = slice(h * size, (h + 1) * size)
        q, k, v, g = query[:, cols], key[:, cols], value[:, cols], msg[:tokens, cols]
        scores = dot(k, q, 1, 1) * factor
        probs = jnp.exp(scores - lse[head0 + h : head0 + h + 1, :] + mask)
        dv[:, cols] = dot(probs.astype(BF16), g, 1, 0)
        dprobs = dot(v, g, 1, 1)
        dscores = (probs * (dprobs - delta_row(msg, tokens, cols))).astype(BF16)
        dk[:, cols] = dot(dscores, q, 1, 0)
        dq[:, cols] = dot(dscores, k, 0, 0) * factor


def own_pair(query, key, value, msg, lse, bias, first, heads):
    tokens = query.shape[0]
    width = msg.shape[1]
    head0 = first // (width // heads)
    part = vmem((tokens, width), lambda i: (0, first // width))
    whole = vmem((tokens, width), lambda i: (0, 0))
    return pl.pallas_call(
        functools.partial(own_kernel, heads, head0),
        grid=(1,),
        in_specs=[part, part, part, vmem(msg.shape, lambda i: (0, 0)), vmem(lse.shape, lambda i: (0, 0)), vmem(bias.shape, lambda i: (0, 0))],
        out_specs=[whole] * 3,
        out_shape=[jax.ShapeDtypeStruct((tokens, width), F32)] * 3,
        compiler_params=params(),
        cost_estimate=cost(10 * tokens * tokens * width, tokens * width * 20, heads * tokens * tokens),
        name="own_pair",
    )(query, key, value, msg, lse, bias)


def cross_kernel(heads, head0, query, key, value, msg, lse, bias, dq, probs_out, dscores_out):
    tokens = query.shape[0]
    size = query.shape[1] // heads
    factor = size ** -0.5
    mask = bias[...]
    for h in range(heads):
        cols = slice(h * size, (h + 1) * size)
        q, k, v, g = query[:, cols], key[:, cols], value[:, cols], msg[:tokens, cols]
        scores = dot(k, q, 1, 1) * factor
        probs = jnp.exp(scores - lse[head0 + h : head0 + h + 1, :] + mask)
        probs_out[:, cols] = probs.astype(BF16)
        dprobs = dot(v, g, 1, 1)
        dscores = (probs * (dprobs - delta_row(msg, tokens, cols))).astype(BF16)
        dscores_out[:, cols] = dscores
        dq[:, cols] = (dot(dscores, k, 0, 0) * factor).astype(BF16)


def cross_pair(query, key, value, msg, lse, bias, first, heads):
    tokens = query.shape[0]
    width = msg.shape[1]
    head0 = first // (width // heads)
    part = vmem((tokens, width), lambda i: (0, first // width))
    whole = vmem((tokens, width), lambda i: (0, 0))
    return pl.pallas_call(
        functools.partial(cross_kernel, heads, head0),
        grid=(1,),
        in_specs=[part, part, part, vmem(msg.shape, lambda i: (0, 0)), vmem(lse.shape, lambda i: (0, 0)), vmem(bias.shape, lambda i: (0, 0))],
        out_specs=[whole] * 3,
        out_shape=[jax.ShapeDtypeStruct((tokens, width), BF16)] * 3,
        compiler_params=params(),
        cost_estimate=cost(6 * tokens * tokens * width, tokens * width * 14, heads * tokens * tokens),
        name="cross_pair",
    )(query, key, value, msg, lse, bias)


def key_kernel(chunks, heads, query, *refs):
    ins, (dk_out, dv_out) = refs[:-2], refs[-2:]
    tokens = query.shape[0]
    size = query.shape[1] // (heads * chunks)
    factor = size ** -0.5
    for c in range(chunks):
        msg, probs, dscores, dk, dv = ins[c * 5 : c * 5 + 5]
        for h in range(heads):
            cols = slice(h * size, (h + 1) * size)
            place = slice((c * heads + h) * size, (c * heads + h + 1) * size)
            dk_out[:, place] = ((dk[:, cols] + dot(dscores[:, cols], query[:, place], 1, 0)) * factor).astype(BF16)
            dv_out[:, place] = (dv[:, cols] + dot(probs[:, cols], msg[:tokens, cols], 1, 0)).astype(BF16)


def key_grads(query, groups, heads):
    tokens, width = query.shape
    return pl.pallas_call(
        functools.partial(key_kernel, len(groups), heads),
        in_specs=[vmem()] * (1 + 5 * len(groups)),
        out_specs=[vmem()] * 2,
        out_shape=[jax.ShapeDtypeStruct((tokens, width), BF16)] * 2,
        compiler_params=params(),
        cost_estimate=cost(4 * tokens * tokens * width, tokens * width * 20),
        name="key_grads",
    )(query, *[a for group in groups for a in group])


def add_kernel(chunks, *refs):
    out = refs[-1]
    width = out.shape[1] // chunks
    for c in range(chunks):
        out[:, c * width : (c + 1) * width] = (refs[2 * c][...] + refs[2 * c + 1][...].astype(F32)).astype(BF16)


def add_all(pairs):
    tokens, width = pairs[0][0].shape
    return pl.pallas_call(
        functools.partial(add_kernel, len(pairs)),
        in_specs=[vmem()] * (2 * len(pairs)),
        out_specs=vmem(),
        out_shape=jax.ShapeDtypeStruct((tokens, width * len(pairs)), BF16),
        compiler_params=params(),
        cost_estimate=cost(2 * tokens * width * len(pairs), 8 * tokens * width * len(pairs)),
        name="query_sum",
    )(*[a for pair in pairs for a in pair])


def on_device(queries, keys, values, out_grad, out_proj, attn_out, log_sum, group_order):
    tokens, width = queries.shape[1:]
    heads = log_sum.shape[1]
    rows = out_proj.shape[0]
    query, key, value, upstream, output = queries[0], keys[0], values[0], out_grad[0], attn_out[0]
    lse = log_sum[0]
    order = group_order[0]
    dp, ctx = lax.axis_size("dp"), lax.axis_size("ctx")
    me, here = lax.axis_index("dp"), lax.axis_index("ctx")
    pair = 2 if dp % 2 == 0 else 1
    chips = dp // pair
    core, chip = me % pair, me // pair

    def along_dp(array, by):
        return lax.ppermute(array, "dp", [(i, (i + by) % dp) for i in range(dp)])

    def along_ctx(array, by):
        return lax.ppermute(array, "ctx", [(i, (i + by) % ctx) for i in range(ctx)])

    def columns_for(there):
        parts = [
            lax.dynamic_slice_in_dim(upstream, (there * pair + (core + i) % pair) * rows, rows, axis=1)
            for i in range(pair)
        ]
        return jnp.concatenate(parts, axis=1)

    arrived = [along_dp(columns_for((chip + j) % chips), pair * j) for j in range(1, chips)]
    weights = [out_proj]
    if pair == 2:
        weights.append(lax.ppermute(out_proj, "dp", [(i, i ^ 1) for i in range(dp)]))
    query_next = along_ctx(query, -1)
    lse_next = along_ctx(lse, -1)
    lhs = [columns_for(chip)] + arrived

    per_block = tokens // GROUP

    def positions(device):
        ids = lax.dynamic_slice_in_dim(order, device * per_block, per_block)
        return (ids[:, None] * GROUP + jnp.arange(GROUP, dtype=jnp.int32)[None, :]).reshape(tokens)

    own_pos = positions(here)
    next_pos = positions((here + 1) % ctx)
    bias_own = jnp.where(own_pos[:, None] <= own_pos[None, :], 0.0, -jnp.inf).astype(F32)
    bias_next = jnp.where(own_pos[:, None] <= next_pos[None, :], 0.0, -jnp.inf).astype(F32)

    chunks = CHUNKS if heads % CHUNKS == 0 else 1
    part = width // chunks
    per = heads // chunks
    groups, sums = [], []
    for c in range(chunks):
        first = c * part
        local, *remote = project(lhs, weights, first, part)
        back = [along_dp(remote[j - 1], -pair * j) for j in range(1, chips)]
        msg = combine(local, back, output, first, per)
        msg_next = along_ctx(msg, -1)
        dq_own, dk_own, dv_own = own_pair(query, key, value, msg, lse, bias_own, first, per)
        dq_cross, probs, dscores = cross_pair(query_next, key, value, msg_next, lse_next, bias_next, first, per)
        groups.append((msg_next, probs, dscores, dk_own, dv_own))
        sums.append((dq_own, along_ctx(dq_cross, 1)))
    key_grad, value_grad = key_grads(query_next, groups, per)
    query_grad = add_all(sums)
    shape = (1, tokens, width)
    return query_grad.reshape(shape), key_grad.reshape(shape), value_grad.reshape(shape)


def solution(mesh):
    return jax.shard_map(
        on_device,
        mesh=mesh,
        in_specs=(
            P("dp", "ctx", None),
            P("dp", "ctx", None),
            P("dp", "ctx", None),
            P("dp", "ctx", None),
            P("dp", None),
            P("dp", "ctx", None),
            P("dp", None, "ctx"),
            P("dp", None),
        ),
        out_specs=(P("dp", "ctx", None), P("dp", "ctx", None), P("dp", "ctx", None)),
        check_vma=False,
    )
```

```python
import functools

import jax
import jax.numpy as jnp
from jax import lax
from jax.experimental import pallas as pl
from jax.experimental.pallas import tpu as pltpu
from jax.sharding import PartitionSpec as P

GROUP = 32
CHUNKS = (8, 8)
REPEAT = False
LANES = 256
EXTRA = 16
VMEM_MIB = 20
F32 = jnp.float32
BF16 = jnp.bfloat16


def dot(a, b, ca, cb):
    return lax.dot_general(a, b, (((ca,), (cb,)), ((), ())), preferred_element_type=F32)


def here_in(space):
    return pl.BlockSpec(memory_space=space)


def pin(array):
    return pltpu.with_memory_space_constraint(array, pltpu.VMEM)


def call(body, name, ins, outs, after=(), scalars=(), free=()):
    n_in, n_after = len(scalars) + len(ins), len(after)

    def kernel(*refs):
        body(refs[:n_in], refs[n_in + n_after :])

    moved = sum(a.size * a.dtype.itemsize for a in ins) + sum(jnp.dtype(t).itemsize * r * c for r, c, t, _ in outs)
    return pl.pallas_call(
        kernel,
        in_specs=[here_in(pltpu.SMEM)] * len(scalars) + [here_in(pltpu.VMEM)] * len(ins) + [here_in(pl.ANY)] * n_after,
        out_specs=[here_in(pltpu.VMEM)] * len(outs),
        out_shape=[pltpu.VMEM((r, c), t) if kept else jax.ShapeDtypeStruct((r, c), t) for r, c, t, kept in outs],
        compiler_params=pltpu.CompilerParams(vmem_limit_bytes=VMEM_MIB * 1024 * 1024),
        cost_estimate=pl.CostEstimate(flops=int(1e9), bytes_accessed=int(1 * moved), transcendentals=0),
        name=name,
    )(*scalars, *[a if i in free else pin(a) for i, a in enumerate(ins)], *after)


def stage(parts, first, width, after=()):
    rows, n, n_after = parts[0].shape[0], len(parts), len(after)

    def kernel(*refs):
        out = refs[n + n_after]

        def copy(semaphores):
            moves = []
            for i in range(n):
                source = refs[i].at[:, pl.ds(first, width)]
                moves.append(pltpu.make_async_copy(source, out.at[:, pl.ds(i * width, width)], semaphores.at[i]))
                moves[i].start()
            for move in moves:
                move.wait()

        pl.run_scoped(copy, pltpu.SemaphoreType.DMA((n,)))

    return pl.pallas_call(
        kernel,
        in_specs=[here_in(pl.ANY)] * (n + n_after),
        out_specs=here_in(pltpu.VMEM),
        out_shape=pltpu.VMEM((rows, n * width), parts[0].dtype),
        compiler_params=pltpu.CompilerParams(vmem_limit_bytes=VMEM_MIB * 1024 * 1024),
        cost_estimate=pl.CostEstimate(flops=int(1e9), bytes_accessed=4 * rows * n * width, transcendentals=0),
        name="stage",
    )(*[pltpu.with_memory_space_constraint(a, pltpu.HBM) for a in parts], *after)


def project(place, sources, weights, first, width, kind, after=()):
    pair = len(weights)
    tokens = sources[0].shape[0]
    rows = weights[0].shape[0]

    def body(ins, outs):
        place, sources, weights = ins[0], ins[1 : 1 + len(sources_in)], ins[1 + len(sources_in) :]
        lhs = []
        for i in range(pair):
            start = (place[0] * pair + (place[1] + i) % pair) * rows
            part = pl.ds(pl.multiple_of(start, rows), rows)
            blocks = [ref[:, part] for ref in sources]
            lhs.append(blocks[0] if len(blocks) == 1 else jnp.concatenate(blocks, axis=0))
        for at in range(0, width, LANES):
            cols = slice(at, at + LANES)
            from_cols = slice(first + at, first + at + LANES)
            total = dot(lhs[0], weights[0][:, from_cols], 1, 0)
            for i in range(1, pair):
                total += dot(lhs[i], weights[i][:, from_cols], 1, 0)
            for j, ref in enumerate(outs):
                ref[:, cols] = total[j * tokens : (j + 1) * tokens].astype(kind)

    sources_in = list(sources)
    return call(
        body, "project", [*sources, *weights], [(tokens, width, kind, True)] * len(sources), after, (place,), (len(sources), len(sources) + 1),
    )


def combine(local, parts, attn_out, lse, first, heads, after=()):
    tokens, width = local.shape
    size = width // heads
    head0 = first // size

    def body(ins, outs):
        local, parts, attn_out, lse = ins[0], ins[1:-2], ins[-2], ins[-1]
        (msg,) = outs
        total = local[...]
        for ref in parts:
            total += ref[...].astype(F32)
        grad = total.astype(BF16)
        msg[:tokens, :] = grad
        product = grad.astype(F32) * attn_out[:, first : first + width].astype(F32)
        high = product.astype(BF16)
        low = (product - high.astype(F32)).astype(BF16)
        ones = jnp.ones((8, size), BF16)
        rows, lses = [], []
        for h in range(heads):
            cols = slice(h * size, (h + 1) * size)
            rows.append(dot(ones, high[:, cols], 1, 1) + dot(ones, low[:, cols], 1, 1))
            lses.append(jnp.broadcast_to(lse[head0 + h : head0 + h + 1, :], (8, tokens)))
        pick = lax.broadcasted_iota(jnp.int32, (8, width), 0)
        both = jnp.where(pick < 3, jnp.concatenate(rows, axis=1), jnp.concatenate(lses, axis=1))
        first_part = both.astype(BF16).astype(F32)
        rest = both - first_part
        second = rest.astype(BF16).astype(F32)
        third = rest - second
        turn = jnp.where(pick < 3, pick, pick - 3)
        kept = jnp.where(turn == 0, first_part, jnp.where(turn == 1, second, third))
        msg[tokens:, :] = jnp.concatenate([kept, kept], axis=0).astype(BF16)

    (msg,) = call(
        body, "combine", [local, *parts, attn_out, lse], [(tokens + EXTRA, width, BF16, True)], after,
    )
    return msg


def rows_of(msg, tokens, cols):
    tail = msg[tokens:, cols].astype(F32)
    return tail[0:1] + tail[1:2] + tail[2:3], tail[3:4] + tail[4:5] + tail[5:6]


def weights_of(q, k, v, g, rows, bias):
    delta, lse = rows
    probs = jnp.exp(dot(k, q, 1, 1) * (q.shape[1] ** -0.5) - lse + bias)
    return probs.astype(BF16), (probs * (dot(v, g, 1, 1) - delta)).astype(BF16)


def places(first, heads, size):
    return [(slice(h * size, (h + 1) * size), slice(first + h * size, first + (h + 1) * size)) for h in range(heads)]


def own_pair(query, key, value, msg, bias, first, heads, before=(), after=()):
    tokens, width = query.shape[0], msg.shape[1]
    size = width // heads
    factor = size ** -0.5

    def body(ins, outs):
        query, key, value, msg, bias = ins[:5]
        dq, dk, dv = outs
        for cols, place in places(first, heads, size):
            q, k, v, g = query[:, place], key[:, place], value[:, place], msg[:tokens, cols]
            rows = rows_of(msg, tokens, cols)
            probs, dscores = weights_of(q, k, v, g, rows, bias[...])
            dv[:, cols] = dot(probs, g, 1, 0)
            dk[:, cols] = dot(dscores, q, 1, 0)
            total = dot(dscores, k, 0, 0)
            if before:
                pairs, bias_before = ins[5:]
                k_old, v_old = pairs[:, cols], pairs[:, slice(width + cols.start, width + cols.stop)]
                _, dscores = weights_of(q, k_old, v_old, g, rows, bias_before[...])
                total += dot(dscores, k_old, 0, 0)
            dq[:, cols] = (total * factor).astype(dq.dtype)

    kind = BF16 if before else F32
    return call(
        body, "own_pair", [query, key, value, msg, bias, *before],
        [(tokens, width, kind, True), (tokens, width, F32, True), (tokens, width, F32, True)], after,
    )


def cross_pair(query, key, value, msg, bias, first, heads, after=()):
    tokens, width = query.shape[0], msg.shape[1]
    size = width // heads
    factor = size ** -0.5

    def body(ins, outs):
        query, key, value, msg, bias = ins
        dq, probs_out, dscores_out = outs
        for cols, place in places(first, heads, size):
            q, k, v, g = query[:, place], key[:, place], value[:, place], msg[:tokens, cols]
            probs, dscores = weights_of(q, k, v, g, rows_of(msg, tokens, cols), bias[...])
            probs_out[:, cols] = probs
            dscores_out[:, cols] = dscores
            dq[:, cols] = (dot(dscores, k, 0, 0) * factor).astype(BF16)

    return call(
        body, "cross_pair", [query, key, value, msg, bias], [(tokens, width, BF16, True)] * 3, after,
    )


def key_grads(query, key, value, bias, groups, plan, after=()):
    tokens, width = query.shape

    def body(ins, outs):
        query, key, value, bias = ins[:4]
        dk_out, dv_out = outs
        at = 4
        for (first, part, heads), group in zip(plan, groups):
            size = part // heads
            factor = size ** -0.5
            refs = ins[at : at + len(group)]
            at += len(group)
            msg, dk, dv = refs[:3]
            for cols, place in places(first, heads, size):
                q, g = query[:, place], msg[:tokens, cols]
                if len(refs) > 3:
                    probs, dscores = refs[3][:, cols], refs[4][:, cols]
                else:
                    rows = rows_of(msg, tokens, cols)
                    probs, dscores = weights_of(q, key[:, place], value[:, place], g, rows, bias[...])
                dk_out[:, place] = ((dk[:, cols] + dot(dscores, q, 1, 0)) * factor).astype(BF16)
                dv_out[:, place] = (dv[:, cols] + dot(probs, g, 1, 0)).astype(BF16)

    return call(
        body, "key_grads", [query, key, value, bias] + [a for group in groups for a in group],
        [(tokens, width, BF16, False)] * 2, after,
    )


def query_grads(groups, plan, after=()):
    tokens, width = groups[0][0].shape[0], sum(part for _, part, _ in plan)

    def body(ins, outs):
        (out,) = outs
        at = 0
        for (first, part, _), group in zip(plan, groups):
            total = ins[at][...]
            if len(group) > 1:
                total = (total + ins[at + 1][...].astype(F32)).astype(BF16)
            out[:, first : first + part] = total
            at += len(group)

    (out,) = call(body, "query_grads", [a for group in groups for a in group], [(tokens, width, BF16, False)], after)
    return out


def on_device(queries, keys, values, out_grad, out_proj, attn_out, log_sum, group_order):
    tokens, width = queries.shape[1:]
    heads = log_sum.shape[1]
    size = width // heads
    rows = out_proj.shape[0]
    query, key, value, upstream, output = queries[0], keys[0], values[0], out_grad[0], attn_out[0]
    lse = log_sum[0]
    order = group_order[0]
    dp, ctx = lax.axis_size("dp"), lax.axis_size("ctx")
    me, here = lax.axis_index("dp"), lax.axis_index("ctx")
    pair = 2 if dp % 2 == 0 else 1
    chips = dp // pair
    core, chip = me % pair, me // pair

    def along_dp(array, by):
        return lax.ppermute(array, "dp", [(i, (i + by) % dp) for i in range(dp)])

    def along_ctx(array, by):
        return lax.ppermute(array, "ctx", [(i, (i + by) % ctx) for i in range(ctx)])

    def columns_for(there):
        return lax.dynamic_slice_in_dim(upstream, there * (pair * rows), pair * rows, axis=1)

    pieces = [columns_for((chip + j) % chips) for j in range(1, chips)]
    arrived = [along_dp(piece, pair * (j + 1)) for j, piece in enumerate(pieces)]
    at_own = jnp.stack([chip, core]).astype(jnp.int32)
    at_cut = jnp.stack([jnp.zeros_like(core), core]).astype(jnp.int32)
    weights = [stage([out_proj], 0, width, pieces)]
    if pair == 2:
        weights.append(lax.ppermute(out_proj, "dp", [(i, i ^ 1) for i in range(dp)]))
    query_sent, _ = lax.optimization_barrier((query, pieces))
    query_next = along_ctx(query_sent, -1)

    per_block = tokens // GROUP

    def positions(device):
        ids = lax.dynamic_slice_in_dim(order, device * per_block, per_block)
        return (ids[:, None] * GROUP + jnp.arange(GROUP, dtype=jnp.int32)[None, :]).reshape(tokens)

    def bias_of(key_block, query_block):
        visible = positions(key_block)[:, None] <= positions(query_block)[None, :]
        return jnp.where(visible, 0.0, -jnp.inf).astype(F32)

    bias_own = bias_of(here, here)
    bias_next = bias_of(here, (here + 1) % ctx)
    bias_before = bias_of((here + ctx - 1) % ctx, here)

    shares = CHUNKS if heads % sum(CHUNKS) == 0 else (1, 0)
    counts = [share * heads // sum(shares) for share in shares]
    plan, done = [], 0
    for count in counts:
        if count:
            plan.append((done * size, count * size, count))
            done += count

    backs, held = [], []
    for first, part, _ in plan:
        remote = project(at_cut, arrived, weights, first, part, BF16, after=held) if arrived else []
        held = list(remote[:1])
        backs.append([along_dp(remote[j - 1], -pair * j) for j in range(1, chips)])

    before = []
    if REPEAT and len(plan) > 1:
        first, part, _ = plan[1]
        before = [along_ctx(stage([key, value], first, part, held), 1)]

    msgs, nexts = [], []
    for c, (first, part, count) in enumerate(plan):
        waits = [query_next] if c == 0 else before + msgs
        (local,) = project(at_own, [upstream], weights, first, part, F32, after=waits + held)
        msgs.append(combine(local, backs[c], output, lse, first, count))
        nexts.append(along_ctx(msgs[c], -1))

    crosses = []
    for c, (first, part, count) in enumerate(plan):
        if not (c and before):
            crosses.append(cross_pair(query_next, key, value, nexts[c], bias_next, first, count))
    sent = [cross[0] for cross in crosses]
    backs = [along_ctx(dq, 1) for dq in sent]
    key_parts, query_parts = [], []
    for c, (first, part, count) in enumerate(plan):
        if c and before:
            extra = (before[0], bias_before)
            own = own_pair(query, key, value, msgs[c], bias_own, first, count, before=extra, after=sent)
            key_parts.append((nexts[c], own[1], own[2]))
            query_parts.append((own[0],))
        else:
            own = own_pair(query, key, value, msgs[c], bias_own, first, count, after=sent)
            key_parts.append((nexts[c], own[1], own[2], crosses[c][1], crosses[c][2]))
            query_parts.append((own[0], backs[c]))
    key_grad, value_grad = key_grads(query_next, key, value, bias_next, key_parts, plan)
    query_grad = query_grads(query_parts, plan)
    shape = (1, tokens, width)
    return query_grad.reshape(shape), key_grad.reshape(shape), value_grad.reshape(shape)


def solution(mesh):
    return jax.shard_map(
        on_device,
        mesh=mesh,
        in_specs=(
            P("dp", "ctx", None),
            P("dp", "ctx", None),
            P("dp", "ctx", None),
            P("dp", "ctx", None),
            P("dp", None),
            P("dp", "ctx", None),
            P("dp", None, "ctx"),
            P("dp", None),
        ),
        out_specs=(P("dp", "ctx", None), P("dp", "ctx", None), P("dp", "ctx", None)),
        check_vma=False,
    )
```

```python
import functools

import jax
import jax.numpy as jnp
from jax import lax
from jax.experimental import pallas as pl
from jax.experimental.pallas import tpu as pltpu
from jax.sharding import PartitionSpec as P

GROUP = 32
CHUNKS = (8, 8)
BOTH = 3
LANES = 256
EXTRA = 8
VMEM_MIB = 20
F32 = jnp.float32
BF16 = jnp.bfloat16


def dot(a, b, ca, cb):
    return lax.dot_general(a, b, (((ca,), (cb,)), ((), ())), preferred_element_type=F32)


def here_in(space):
    return pl.BlockSpec(memory_space=space)


def pin(array):
    return pltpu.with_memory_space_constraint(array, pltpu.VMEM)


def call(body, name, ins, outs, after=(), scalars=(), free=()):
    n_in, n_after = len(scalars) + len(ins), len(after)

    def kernel(*refs):
        body(refs[:n_in], refs[n_in + n_after :])

    moved = sum(a.size * a.dtype.itemsize for a in ins) + sum(jnp.dtype(t).itemsize * r * c for r, c, t, _ in outs)
    return pl.pallas_call(
        kernel,
        in_specs=[here_in(pltpu.SMEM)] * len(scalars) + [here_in(pltpu.VMEM)] * len(ins) + [here_in(pl.ANY)] * n_after,
        out_specs=[here_in(pltpu.VMEM)] * len(outs),
        out_shape=[pltpu.VMEM((r, c), t) if kept else jax.ShapeDtypeStruct((r, c), t) for r, c, t, kept in outs],
        compiler_params=pltpu.CompilerParams(vmem_limit_bytes=VMEM_MIB * 1024 * 1024),
        cost_estimate=pl.CostEstimate(flops=int(1e9), bytes_accessed=int(1 * moved), transcendentals=0),
        name=name,
    )(*scalars, *[a if i in free else pin(a) for i, a in enumerate(ins)], *after)


def stage(parts, first, width, after=()):
    rows, n, n_after = parts[0].shape[0], len(parts), len(after)
    cuts = 4 if rows % 64 == 0 else 1
    height = rows // cuts

    def kernel(*refs):
        out = refs[n + n_after]

        def copy(semaphores):
            moves = []
            for i in range(n):
                for j in range(cuts):
                    lines = pl.ds(j * height, height)
                    source = refs[i].at[lines, pl.ds(first, width)]
                    target = out.at[lines, pl.ds(i * width, width)]
                    moves.append(pltpu.make_async_copy(source, target, semaphores.at[i * cuts + j]))
                    moves[-1].start()
            for move in moves:
                move.wait()

        pl.run_scoped(copy, pltpu.SemaphoreType.DMA((n * cuts,)))

    return pl.pallas_call(
        kernel,
        in_specs=[here_in(pl.ANY)] * (n + n_after),
        out_specs=here_in(pltpu.VMEM),
        out_shape=pltpu.VMEM((rows, n * width), parts[0].dtype),
        compiler_params=pltpu.CompilerParams(vmem_limit_bytes=VMEM_MIB * 1024 * 1024),
        cost_estimate=pl.CostEstimate(flops=int(1e9), bytes_accessed=4 * rows * n * width, transcendentals=0),
        name="stage",
    )(*[pltpu.with_memory_space_constraint(a, pltpu.HBM) for a in parts], *after)


def project(place, sources, weights, first, width, kind, after=()):
    pair = len(weights)
    tokens = sources[0].shape[0]
    rows = weights[0].shape[0]

    def body(ins, outs):
        place, sources, weights = ins[0], ins[1 : 1 + len(sources_in)], ins[1 + len(sources_in) :]
        lhs = []
        for i in range(pair):
            start = (place[0] * pair + (place[1] + i) % pair) * rows
            part = pl.ds(pl.multiple_of(start, rows), rows)
            blocks = [ref[:, part] for ref in sources]
            lhs.append(blocks[0] if len(blocks) == 1 else jnp.concatenate(blocks, axis=0))
        for at in range(0, width, LANES):
            cols = slice(at, at + LANES)
            from_cols = slice(first + at, first + at + LANES)
            total = dot(lhs[0], weights[0][:, from_cols], 1, 0)
            for i in range(1, pair):
                total += dot(lhs[i], weights[i][:, from_cols], 1, 0)
            for j, ref in enumerate(outs):
                ref[:, cols] = total[j * tokens : (j + 1) * tokens].astype(kind)

    sources_in = list(sources)
    return call(
        body, "project", [*sources, *weights], [(tokens, width, kind, True)] * len(sources), after, (place,), (len(sources), len(sources) + 1),
    )


def combine(local, parts, attn_out, lse, first, heads, after=()):
    tokens, width = local.shape
    size = width // heads
    head0 = first // size

    def body(ins, outs):
        local, parts, attn_out, lse = ins[0], ins[1:-2], ins[-2], ins[-1]
        (msg,) = outs
        total = local[...]
        for ref in parts:
            total += ref[...].astype(F32)
        grad = total.astype(BF16)
        msg[:tokens, :] = grad
        product = grad.astype(F32) * attn_out[:, first : first + width].astype(F32)
        high = product.astype(BF16)
        low = (product - high.astype(F32)).astype(BF16)
        ones = jnp.ones((8, size), BF16)
        rows, lses = [], []
        for h in range(heads):
            cols = slice(h * size, (h + 1) * size)
            rows.append(dot(ones, high[:, cols], 1, 1) + dot(ones, low[:, cols], 1, 1))
            lses.append(jnp.broadcast_to(lse[head0 + h : head0 + h + 1, :], (8, tokens)))
        pick = lax.broadcasted_iota(jnp.int32, (8, width), 0)
        both = jnp.where(pick < 3, jnp.concatenate(rows, axis=1), jnp.concatenate(lses, axis=1))
        first_part = both.astype(BF16).astype(F32)
        rest = both - first_part
        second = rest.astype(BF16).astype(F32)
        third = rest - second
        turn = jnp.where(pick < 3, pick, pick - 3)
        kept = jnp.where(turn == 0, first_part, jnp.where(turn == 1, second, third))
        msg[tokens:, :] = kept.astype(BF16)

    (msg,) = call(
        body, "combine", [local, *parts, attn_out, lse], [(tokens + EXTRA, width, BF16, True)], after,
    )
    return msg


def rows_of(msg, tokens, cols):
    tail = msg[tokens:, cols].astype(F32)
    return tail[0:1] + tail[1:2] + tail[2:3], tail[3:4] + tail[4:5] + tail[5:6]


def weights_of(q, k, v, g, rows, bias):
    delta, lse = rows
    probs = jnp.exp(dot(k, q, 1, 1) * (q.shape[1] ** -0.5) - lse + bias)
    return probs.astype(BF16), (probs * (dot(v, g, 1, 1) - delta)).astype(BF16)


def places(first, heads, size):
    return [(slice(h * size, (h + 1) * size), slice(first + h * size, first + (h + 1) * size)) for h in range(heads)]


def own_pair(query, key, value, msg, bias, first, heads, extra=0, before=(), after=()):
    tokens, width = query.shape[0], msg.shape[1]
    size = width // heads
    factor = size ** -0.5

    def body(ins, outs):
        query, key, value, msg, bias = ins[:5]
        dq, dk, dv = outs
        for h, (cols, place) in enumerate(places(first, heads, size)):
            q, k, v, g = query[:, place], key[:, place], value[:, place], msg[:tokens, cols]
            rows = rows_of(msg, tokens, cols)
            probs, dscores = weights_of(q, k, v, g, rows, bias[...])
            dv[:, cols] = dot(probs, g, 1, 0)
            dk[:, cols] = dot(dscores, q, 1, 0)
            total = dot(dscores, k, 0, 0)
            if h >= heads - extra:
                pairs, bias_before = ins[5:]
                at = (h - (heads - extra)) * size
                k_old, v_old = pairs[:, at : at + size], pairs[:, extra * size + at : extra * size + at + size]
                _, dscores = weights_of(q, k_old, v_old, g, rows, bias_before[...])
                total += dot(dscores, k_old, 0, 0)
            dq[:, cols] = total * factor

    return call(
        body, "own_pair", [query, key, value, msg, bias, *before], [(tokens, width, F32, True)] * 3, after,
    )


def cross_pair(query, key, value, msg, bias, first, heads, size, after=()):
    tokens, width = query.shape[0], heads * size
    factor = size ** -0.5

    def body(ins, outs):
        query, key, value, msg, bias = ins
        dq, probs_out, dscores_out = outs
        for cols, place in places(first, heads, size):
            q, k, v, g = query[:, place], key[:, place], value[:, place], msg[:tokens, cols]
            probs, dscores = weights_of(q, k, v, g, rows_of(msg, tokens, cols), bias[...])
            probs_out[:, cols] = probs
            dscores_out[:, cols] = dscores
            dq[:, cols] = (dot(dscores, k, 0, 0) * factor).astype(BF16)

    return call(
        body, "cross_pair", [query, key, value, msg, bias], [(tokens, width, BF16, True)] * 3, after,
    )


def key_grads(query, key, value, bias, groups, plan, after=()):
    tokens, width = query.shape

    def body(ins, outs):
        query, key, value, bias = ins[:4]
        dk_out, dv_out = outs
        at = 4
        for (first, part, heads, extra), group in zip(plan, groups):
            size = part // heads
            factor = size ** -0.5
            msg, dk, dv = ins[at : at + 3]
            known = ins[at + 3 : at + len(group)]
            at += len(group)
            for h, (cols, place) in enumerate(places(first, heads, size)):
                q, g = query[:, place], msg[:tokens, cols]
                if h < heads - extra:
                    probs, dscores = known[0][:, cols], known[1][:, cols]
                else:
                    rows = rows_of(msg, tokens, cols)
                    probs, dscores = weights_of(q, key[:, place], value[:, place], g, rows, bias[...])
                dk_out[:, place] = ((dk[:, cols] + dot(dscores, q, 1, 0)) * factor).astype(BF16)
                dv_out[:, place] = (dv[:, cols] + dot(probs, g, 1, 0)).astype(BF16)

    return call(
        body, "key_grads", [query, key, value, bias] + [a for group in groups for a in group],
        [(tokens, width, BF16, False)] * 2, after,
    )


def query_grads(owns, backs, plan, after=()):
    tokens, width = owns[0].shape[0], sum(step[1] for step in plan)

    def body(ins, outs):
        (out,) = outs
        owns, backs = ins[: len(plan)], list(ins[len(plan) :])
        for (first, part, heads, extra), own in zip(plan, owns):
            sent = part - extra * (part // heads)
            if sent:
                out[:, first : first + sent] = (own[:, :sent] + backs.pop(0)[...].astype(F32)).astype(BF16)
            if extra:
                out[:, first + sent : first + part] = own[:, sent:].astype(BF16)

    (out,) = call(body, "query_grads", [*owns, *backs], [(tokens, width, BF16, False)], after)
    return out


def on_device(queries, keys, values, out_grad, out_proj, attn_out, log_sum, group_order):
    tokens, width = queries.shape[1:]
    heads = log_sum.shape[1]
    size = width // heads
    rows = out_proj.shape[0]
    query, key, value, upstream, output = queries[0], keys[0], values[0], out_grad[0], attn_out[0]
    lse = log_sum[0]
    order = group_order[0]
    dp, ctx = lax.axis_size("dp"), lax.axis_size("ctx")
    me, here = lax.axis_index("dp"), lax.axis_index("ctx")
    pair = 2 if dp % 2 == 0 else 1
    chips = dp // pair
    core, chip = me % pair, me // pair

    def along_dp(array, by):
        return lax.ppermute(array, "dp", [(i, (i + by) % dp) for i in range(dp)])

    def along_ctx(array, by):
        return lax.ppermute(array, "ctx", [(i, (i + by) % ctx) for i in range(ctx)])

    def columns_for(there):
        return lax.dynamic_slice_in_dim(upstream, there * (pair * rows), pair * rows, axis=1)

    pieces = [columns_for((chip + j) % chips) for j in range(1, chips)]
    arrived = [along_dp(piece, pair * (j + 1)) for j, piece in enumerate(pieces)]
    at_own = jnp.stack([chip, core]).astype(jnp.int32)
    at_cut = jnp.stack([jnp.zeros_like(core), core]).astype(jnp.int32)
    weights = [stage([out_proj], 0, width, pieces)]
    if pair == 2:
        weights.append(stage([lax.ppermute(out_proj, "dp", [(i, i ^ 1) for i in range(dp)])], 0, width))
    query_sent, _ = lax.optimization_barrier((query, pieces))
    query_next = along_ctx(query_sent, -1)

    per_block = tokens // GROUP

    def positions(device):
        ids = lax.dynamic_slice_in_dim(order, device * per_block, per_block)
        return (ids[:, None] * GROUP + jnp.arange(GROUP, dtype=jnp.int32)[None, :]).reshape(tokens)

    def bias_of(key_block, query_block):
        visible = positions(key_block)[:, None] <= positions(query_block)[None, :]
        return jnp.where(visible, 0.0, -jnp.inf).astype(F32)

    bias_own = bias_of(here, here)
    bias_next = bias_of(here, (here + 1) % ctx)
    bias_before = bias_of((here + ctx - 1) % ctx, here)

    shares = CHUNKS if heads == sum(CHUNKS) else (heads,)
    plan, done = [], 0
    for c, count in enumerate(shares):
        plan.append((done * size, count * size, count, BOTH if c > 0 and c == len(shares) - 1 else 0))
        done += count

    backs, held = [], []
    for first, part, _, _ in plan:
        remote = project(at_cut, arrived, weights, first, part, BF16, after=held) if arrived else []
        held = list(remote[:1])
        backs.append([along_dp(remote[j - 1], -pair * j) for j in range(1, chips)])

    extra = plan[-1][3]
    before = []
    if extra:
        before = [along_ctx(stage([key, value], width - extra * size, extra * size, held), 1)]

    msgs, nexts = [], []
    for c, (first, part, count, _) in enumerate(plan):
        waits = [query_next] if c == 0 else msgs
        (local,) = project(at_own, [upstream], weights, first, part, F32, after=waits + held)
        msgs.append(combine(local, backs[c], output, lse, first, count, after=before if c else []))
        nexts.append(along_ctx(msgs[c], -1))

    crosses, sent, owns = [], [], []
    for c, (first, part, count, extra) in enumerate(plan):
        cross = ()
        if count > extra:
            waits = sent[-1:] + [own[0] for own in owns[-1:]]
            cross = cross_pair(query_next, key, value, nexts[c], bias_next, first, count - extra, size, after=waits)
            sent.append(cross[0])
        crosses.append(cross)
        both = (before[0], bias_before) if extra else ()
        owns.append(own_pair(query, key, value, msgs[c], bias_own, first, count, extra, both, after=sent[-1:]))
    returned = [along_ctx(dq, 1) for dq in sent]
    key_parts = [(nexts[c], own[1], own[2], *crosses[c][1:]) for c, own in enumerate(owns)]
    owns = [own[0] for own in owns]
    key_grad, value_grad = key_grads(query_next, key, value, bias_next, key_parts, plan)
    query_grad = query_grads(owns, returned, plan)
    shape = (1, tokens, width)
    return query_grad.reshape(shape), key_grad.reshape(shape), value_grad.reshape(shape)


def solution(mesh):
    return jax.shard_map(
        on_device,
        mesh=mesh,
        in_specs=(
            P("dp", "ctx", None),
            P("dp", "ctx", None),
            P("dp", "ctx", None),
            P("dp", "ctx", None),
            P("dp", None),
            P("dp", "ctx", None),
            P("dp", None, "ctx"),
            P("dp", None),
        ),
        out_specs=(P("dp", "ctx", None), P("dp", "ctx", None), P("dp", "ctx", None)),
        check_vma=False,
    )
```

```python
import functools

import jax
import jax.numpy as jnp
from jax import lax
from jax.experimental import pallas as pl
from jax.experimental.pallas import tpu as pltpu
from jax.sharding import PartitionSpec as P

GROUP = 32
CHUNKS = ((8,), (5, 3))
BOTH = 3
LANES = 256
EARLY = False
EXTRA = 8
VMEM_MIB = 20
F32 = jnp.float32
BF16 = jnp.bfloat16


def dot(a, b, ca, cb):
    return lax.dot_general(a, b, (((ca,), (cb,)), ((), ())), preferred_element_type=F32)


def here_in(space):
    return pl.BlockSpec(memory_space=space)


def pin(array):
    return pltpu.with_memory_space_constraint(array, pltpu.VMEM)


def call(body, name, ins, outs, after=(), scalars=(), free=()):
    n_in, n_after = len(scalars) + len(ins), len(after)

    def kernel(*refs):
        body(refs[:n_in], refs[n_in + n_after :])

    moved = sum(a.size * a.dtype.itemsize for a in ins) + sum(jnp.dtype(t).itemsize * r * c for r, c, t, _ in outs)
    return pl.pallas_call(
        kernel,
        in_specs=[here_in(pltpu.SMEM)] * len(scalars) + [here_in(pltpu.VMEM)] * len(ins) + [here_in(pl.ANY)] * n_after,
        out_specs=[here_in(pltpu.VMEM)] * len(outs),
        out_shape=[pltpu.VMEM((r, c), t) if kept else jax.ShapeDtypeStruct((r, c), t) for r, c, t, kept in outs],
        compiler_params=pltpu.CompilerParams(vmem_limit_bytes=VMEM_MIB * 1024 * 1024),
        cost_estimate=pl.CostEstimate(flops=int(1e9), bytes_accessed=int(1 * moved), transcendentals=0),
        name=name,
    )(*scalars, *[a if i in free else pin(a) for i, a in enumerate(ins)], *after)


def stage(parts, first, width, after=()):
    rows, n, n_after = parts[0].shape[0], len(parts), len(after)
    cuts = 4 if rows % 64 == 0 else 1
    height = rows // cuts

    def kernel(*refs):
        out = refs[n + n_after]

        def copy(semaphores):
            moves = []
            for i in range(n):
                for j in range(cuts):
                    lines = pl.ds(j * height, height)
                    source = refs[i].at[lines, pl.ds(first, width)]
                    target = out.at[lines, pl.ds(i * width, width)]
                    moves.append(pltpu.make_async_copy(source, target, semaphores.at[i * cuts + j]))
                    moves[-1].start()
            for move in moves:
                move.wait()

        pl.run_scoped(copy, pltpu.SemaphoreType.DMA((n * cuts,)))

    return pl.pallas_call(
        kernel,
        in_specs=[here_in(pl.ANY)] * (n + n_after),
        out_specs=here_in(pltpu.VMEM),
        out_shape=pltpu.VMEM((rows, n * width), parts[0].dtype),
        compiler_params=pltpu.CompilerParams(vmem_limit_bytes=VMEM_MIB * 1024 * 1024),
        cost_estimate=pl.CostEstimate(flops=int(1e9), bytes_accessed=4 * rows * n * width, transcendentals=0),
        name="stage",
    )(*[pltpu.with_memory_space_constraint(a, pltpu.HBM) for a in parts], *after)


def project(place, sources, weights, first, width, kind, after=()):
    pair = len(weights)
    tokens = sources[0].shape[0]
    rows = weights[0].shape[0]

    def body(ins, outs):
        place, sources, weights = ins[0], ins[1 : 1 + len(sources_in)], ins[1 + len(sources_in) :]
        lhs = []
        for i in range(pair):
            start = (place[0] * pair + (place[1] + i) % pair) * rows
            part = pl.ds(pl.multiple_of(start, rows), rows)
            blocks = [ref[:, part] for ref in sources]
            lhs.append(blocks[0] if len(blocks) == 1 else jnp.concatenate(blocks, axis=0))
        for at in range(0, width, LANES):
            cols = slice(at, at + LANES)
            from_cols = slice(first + at, first + at + LANES)
            total = dot(lhs[0], weights[0][:, from_cols], 1, 0)
            for i in range(1, pair):
                total += dot(lhs[i], weights[i][:, from_cols], 1, 0)
            for j, ref in enumerate(outs):
                ref[:, cols] = total[j * tokens : (j + 1) * tokens].astype(kind)

    sources_in = list(sources)
    return call(
        body, "project", [*sources, *weights], [(tokens, width, kind, True)] * len(sources), after, (place,), (len(sources), len(sources) + 1),
    )


def combine(local, parts, attn_out, lse, first, cuts, size, after=()):
    tokens, width = local.shape
    head0 = first // size

    def body(ins, outs):
        local, parts, attn_out, lse = ins[0], ins[1:-2], ins[-2], ins[-1]
        done = 0
        for msg, heads in zip(outs, cuts):
            here = slice(done * size, (done + heads) * size)
            place = slice(first + here.start, first + here.stop)
            total = local[:, here]
            for ref in parts:
                total += ref[:, here].astype(F32)
            grad = total.astype(BF16)
            msg[:tokens, :] = grad
            product = grad.astype(F32) * attn_out[:, place].astype(F32)
            high = product.astype(BF16)
            low = (product - high.astype(F32)).astype(BF16)
            ones = jnp.ones((8, size), BF16)
            rows, lses = [], []
            for h in range(heads):
                cols = slice(h * size, (h + 1) * size)
                line = slice(head0 + done + h, head0 + done + h + 1)
                rows.append(dot(ones, high[:, cols], 1, 1) + dot(ones, low[:, cols], 1, 1))
                lses.append(jnp.broadcast_to(lse[line, :], (8, tokens)))
            pick = lax.broadcasted_iota(jnp.int32, (8, heads * size), 0)
            both = jnp.where(pick < 3, jnp.concatenate(rows, axis=1), jnp.concatenate(lses, axis=1))
            first_part = both.astype(BF16).astype(F32)
            rest = both - first_part
            second = rest.astype(BF16).astype(F32)
            third = rest - second
            turn = jnp.where(pick < 3, pick, pick - 3)
            kept = jnp.where(turn == 0, first_part, jnp.where(turn == 1, second, third))
            msg[tokens:, :] = kept.astype(BF16)
            done += heads

    return call(
        body, "combine", [local, *parts, attn_out, lse],
        [(tokens + EXTRA, heads * size, BF16, True) for heads in cuts], after,
    )


def rows_of(msg, tokens, cols):
    tail = msg[tokens:, cols].astype(F32)
    return tail[0:1] + tail[1:2] + tail[2:3], tail[3:4] + tail[4:5] + tail[5:6]


def bias_of(order, key_block, query_block, tokens):
    def position(block, axis):
        at = lax.broadcasted_iota(jnp.int32, (tokens, tokens), axis)
        count = tokens // GROUP
        base = jnp.full((tokens, tokens), order[block * count] * GROUP, jnp.int32)
        for g in range(1, count):
            base = jnp.where(at >= g * GROUP, (order[block * count + g] - g) * GROUP, base)
        return base + at

    return jnp.where(position(key_block, 0) <= position(query_block, 1), 0.0, -jnp.inf).astype(F32)


def masks(scalars, tokens, after=()):
    def body(ins, outs):
        order, spots = ins
        for out, (key_block, query_block) in zip(outs, ((0, 0), (0, 1), (2, 0))):
            out[...] = bias_of(order, spots[key_block], spots[query_block], tokens)

    return call(body, "masks", [], [(tokens, tokens, F32, True)] * 3, after, scalars)


def weights_of(q, k, v, g, rows, bias):
    delta, lse = rows
    probs = jnp.exp(dot(k, q, 1, 1) * (q.shape[1] ** -0.5) - lse + bias)
    return probs.astype(BF16), (probs * (dot(v, g, 1, 1) - delta)).astype(BF16)


def places(first, heads, size):
    return [(slice(h * size, (h + 1) * size), slice(first + h * size, first + (h + 1) * size)) for h in range(heads)]


def own_pair(query, key, value, bias, msgs, first, size, extra=0, before=(), after=()):
    tokens = query.shape[0]
    width = sum(msg.shape[1] for msg in msgs)
    factor = size ** -0.5

    def body(ins, outs):
        query, key, value, bias = ins[:4]
        msgs_in, pairs = ins[4 : 4 + len(msgs)], ins[4 + len(msgs) :]
        dq, dk, dv = outs
        done = 0
        for msg in msgs_in:
            for cols, _ in places(0, msg.shape[1] // size, size):
                here = slice(done, done + size)
                place = slice(first + done, first + done + size)
                q, k, v, g = query[:, place], key[:, place], value[:, place], msg[:tokens, cols]
                rows = rows_of(msg, tokens, cols)
                probs, dscores = weights_of(q, k, v, g, rows, bias[...])
                dv[:, here] = dot(probs, g, 1, 0)
                dk[:, here] = dot(dscores, q, 1, 0)
                total = dot(dscores, k, 0, 0)
                at = done - (width - extra * size)
                if at >= 0:
                    k_old = pairs[0][:, at : at + size]
                    v_old = pairs[0][:, extra * size + at : extra * size + at + size]
                    _, dscores = weights_of(q, k_old, v_old, g, rows, pairs[1][...])
                    total += dot(dscores, k_old, 0, 0)
                dq[:, here] = total * factor
                done += size

    return call(
        body, "own_pair", [query, key, value, bias, *msgs, *before], [(tokens, width, F32, True)] * 3, after,
    )


def cross_pair(query, key, value, bias, msg, first, heads, size, after=()):
    tokens, width = query.shape[0], heads * size
    factor = size ** -0.5

    def body(ins, outs):
        query, key, value, bias, msg = ins
        dq, probs_out, dscores_out = outs
        for cols, place in places(first, heads, size):
            q, k, v, g = query[:, place], key[:, place], value[:, place], msg[:tokens, cols]
            probs, dscores = weights_of(q, k, v, g, rows_of(msg, tokens, cols), bias[...])
            probs_out[:, cols] = probs
            dscores_out[:, cols] = dscores
            dq[:, cols] = (dot(dscores, k, 0, 0) * factor).astype(BF16)

    return call(
        body, "cross_pair", [query, key, value, bias, msg], [(tokens, width, BF16, True)] * 3, after,
    )


def key_grads(query, key, value, bias, nexts, owns, knowns, plan, after=()):
    tokens, width = query.shape

    def body(ins, outs):
        query, key, value, bias = ins[:4]
        refs = list(ins[4:])
        dk_out, dv_out = outs
        msgs = [refs.pop(0) for _ in nexts]
        sums = [[refs.pop(0) for _ in own] for own in owns]
        pairs = [[refs.pop(0) for _ in known] for known in knowns]
        for (first, part, heads, extra, step, offset), msg, known in zip(plan, msgs, pairs):
            size = part // heads
            factor = size ** -0.5
            dk, dv = sums[step]
            for h, (cols, place) in enumerate(places(first, heads, size)):
                here = slice(offset + cols.start, offset + cols.stop)
                q, g = query[:, place], msg[:tokens, cols]
                if h < heads - extra:
                    probs, dscores = known[0][:, cols], known[1][:, cols]
                else:
                    rows = rows_of(msg, tokens, cols)
                    probs, dscores = weights_of(q, key[:, place], value[:, place], g, rows, bias[...])
                dk_out[:, place] = ((dk[:, here] + dot(dscores, q, 1, 0)) * factor).astype(BF16)
                dv_out[:, place] = (dv[:, here] + dot(probs, g, 1, 0)).astype(BF16)

    flat = [a for group in (*owns, *knowns) for a in group]
    return call(
        body, "key_grads", [query, key, value, bias, *nexts, *flat], [(tokens, width, BF16, False)] * 2, after,
    )


def query_grads(owns, backs, plan, after=()):
    tokens, width = owns[0].shape[0], sum(step[1] for step in plan)

    def body(ins, outs):
        (out,) = outs
        owns_in, backs_in = ins[: len(owns)], list(ins[len(owns) :])
        for first, part, heads, extra, step, offset in plan:
            sent = part - extra * (part // heads)
            own = owns_in[step]
            if sent:
                out[:, first : first + sent] = (own[:, offset : offset + sent] + backs_in.pop(0)[...].astype(F32)).astype(BF16)
            if extra:
                out[:, first + sent : first + part] = own[:, offset + sent : offset + part].astype(BF16)

    (out,) = call(body, "query_grads", [*owns, *backs], [(tokens, width, BF16, False)], after)
    return out


def on_device(queries, keys, values, out_grad, out_proj, attn_out, log_sum, group_order):
    tokens, width = queries.shape[1:]
    heads = log_sum.shape[1]
    size = width // heads
    rows = out_proj.shape[0]
    query, key, value, upstream, output = queries[0], keys[0], values[0], out_grad[0], attn_out[0]
    lse = log_sum[0]
    dp, ctx = lax.axis_size("dp"), lax.axis_size("ctx")
    me, here = lax.axis_index("dp"), lax.axis_index("ctx")
    pair = 2 if dp % 2 == 0 else 1
    chips = dp // pair
    core, chip = me % pair, me // pair

    def along_dp(array, by):
        return lax.ppermute(array, "dp", [(i, (i + by) % dp) for i in range(dp)])

    def along_ctx(array, by):
        return lax.ppermute(array, "ctx", [(i, (i + by) % ctx) for i in range(ctx)])

    def columns_for(there):
        return lax.dynamic_slice_in_dim(upstream, there * (pair * rows), pair * rows, axis=1)

    pieces = [columns_for((chip + j) % chips) for j in range(1, chips)]
    arrived = [along_dp(piece, pair * (j + 1)) for j, piece in enumerate(pieces)]
    at_own = jnp.stack([chip, core]).astype(jnp.int32)
    at_cut = jnp.stack([jnp.zeros_like(core), core]).astype(jnp.int32)
    weights = [stage([out_proj], 0, width, pieces)]
    if pair == 2:
        weights.append(stage([lax.ppermute(out_proj, "dp", [(i, i ^ 1) for i in range(dp)])], 0, width))
    query_sent, _ = lax.optimization_barrier((query, pieces))
    query_next = along_ctx(query_sent, -1)

    order = group_order[0]
    spots = jnp.stack([here, (here + 1) % ctx, (here + ctx - 1) % ctx]).astype(jnp.int32)
    scalars = (order, spots)

    chunks = CHUNKS if heads == sum(sum(cuts) for cuts in CHUNKS) else ((heads,),)
    both = BOTH if chunks is CHUNKS else 0
    plan, steps, done = [], [], 0
    for cuts in chunks:
        steps.append((done * size, sum(cuts) * size, cuts))
        for count in cuts:
            plan.append((done * size, count * size, count, 0, len(steps) - 1, done * size - steps[-1][0]))
            done += count
    plan[-1] = (*plan[-1][:3], both, *plan[-1][4:])

    backs, held = [], []
    for first, part, _ in steps:
        remote = project(at_cut, arrived, weights, first, part, BF16, after=held) if arrived else []
        held = list(remote[:1])
        backs.append([along_dp(remote[j - 1], -pair * j) for j in range(1, chips)])

    extra = plan[-1][3]
    before = []
    if extra:
        before = [along_ctx(stage([key, value], width - extra * size, extra * size, held), 1)]

    bias_own, bias_next, bias_before = masks(scalars, tokens, held)
    locals_ = []
    if EARLY:
        for c, (first, part, cuts) in enumerate(steps):
            waits = [query_next] if c == 0 else locals_[-1:]
            locals_ += project(at_own, [upstream], weights, first, part, F32, after=waits + held)
    msgs = []
    for c, (first, part, cuts) in enumerate(steps):
        if not EARLY:
            waits = [query_next] if c == 0 else msgs[-1]
            locals_ += project(at_own, [upstream], weights, first, part, F32, after=list(waits) + held)
        waits = (before if c else []) + locals_[c + 1 :]
        msgs.append(combine(locals_[c], backs[c], output, lse, first, cuts, size, after=waits))
    nexts = [along_ctx(msg, -1) for group in msgs for msg in group]

    crosses, sent, owns = [], [], []
    for c, (first, part, count, extra, step, _) in enumerate(plan):
        cross = ()
        if count > extra:
            waits = sent[-1:] + [own[0] for own in owns[-1:]]
            cross = cross_pair(query_next, key, value, bias_next, nexts[c], first, count - extra, size, after=waits)
            sent.append(cross[0])
        crosses.append(cross[1:])
        if c + 1 == len(plan) or plan[c + 1][4] > step:
            last = c + 1 == len(plan) and extra
            owns.append(
                own_pair(
                    query, key, value, bias_own, msgs[step], steps[step][0], size, extra if last else 0,
                    (*before, bias_before) if last else (), after=sent[-1:],
                )
            )
    returned = [along_ctx(dq, 1) for dq in sent]
    sums = [own[1:] for own in owns]
    key_grad, value_grad = key_grads(query_next, key, value, bias_next, nexts, sums, crosses, plan)
    query_grad = query_grads([own[0] for own in owns], returned, plan)
    shape = (1, tokens, width)
    return query_grad.reshape(shape), key_grad.reshape(shape), value_grad.reshape(shape)


def solution(mesh):
    return jax.shard_map(
        on_device,
        mesh=mesh,
        in_specs=(
            P("dp", "ctx", None),
            P("dp", "ctx", None),
            P("dp", "ctx", None),
            P("dp", "ctx", None),
            P("dp", None),
            P("dp", "ctx", None),
            P("dp", None, "ctx"),
            P("dp", None),
        ),
        out_specs=(P("dp", "ctx", None), P("dp", "ctx", None), P("dp", "ctx", None)),
        check_vma=False,
    )
```

```python
import functools

import jax
import jax.numpy as jnp
from jax import lax
from jax.experimental import pallas as pl
from jax.experimental.pallas import tpu as pltpu
from jax.sharding import PartitionSpec as P

GROUP = 32
CHUNKS = ((8,), (5, 3))
BOTH = 3
LANES = 256
EXTRA = 16
VMEM_MIB = 20
F32 = jnp.float32
BF16 = jnp.bfloat16


def dot(a, b, ca, cb):
    return lax.dot_general(a, b, (((ca,), (cb,)), ((), ())), preferred_element_type=F32)


def here_in(space):
    return pl.BlockSpec(memory_space=space)


def pin(array):
    return pltpu.with_memory_space_constraint(array, pltpu.VMEM)


def call(body, name, ins, outs, after=(), scalars=(), free=()):
    n_in, n_after = len(scalars) + len(ins), len(after)

    def kernel(*refs):
        body(refs[:n_in], refs[n_in + n_after :])

    moved = sum(a.size * a.dtype.itemsize for a in ins) + sum(jnp.dtype(t).itemsize * r * c for r, c, t, _ in outs)
    return pl.pallas_call(
        kernel,
        in_specs=[here_in(pltpu.SMEM)] * len(scalars) + [here_in(pltpu.VMEM)] * len(ins) + [here_in(pl.ANY)] * n_after,
        out_specs=[here_in(pltpu.VMEM)] * len(outs),
        out_shape=[pltpu.VMEM((r, c), t) if kept else jax.ShapeDtypeStruct((r, c), t) for r, c, t, kept in outs],
        compiler_params=pltpu.CompilerParams(vmem_limit_bytes=VMEM_MIB * 1024 * 1024),
        cost_estimate=pl.CostEstimate(flops=int(1e9), bytes_accessed=int(1 * moved), transcendentals=0),
        name=name,
    )(*scalars, *[a if i in free else pin(a) for i, a in enumerate(ins)], *after)


def stage(parts, first, width, after=()):
    rows, n, n_after = parts[0].shape[0], len(parts), len(after)
    cuts = 4 if rows % 64 == 0 else 1
    height = rows // cuts

    def kernel(*refs):
        out = refs[n + n_after]

        def copy(semaphores):
            moves = []
            for i in range(n):
                for j in range(cuts):
                    lines = pl.ds(j * height, height)
                    source = refs[i].at[lines, pl.ds(first, width)]
                    target = out.at[lines, pl.ds(i * width, width)]
                    moves.append(pltpu.make_async_copy(source, target, semaphores.at[i * cuts + j]))
                    moves[-1].start()
            for move in moves:
                move.wait()

        pl.run_scoped(copy, pltpu.SemaphoreType.DMA((n * cuts,)))

    return pl.pallas_call(
        kernel,
        in_specs=[here_in(pl.ANY)] * (n + n_after),
        out_specs=here_in(pltpu.VMEM),
        out_shape=pltpu.VMEM((rows, n * width), parts[0].dtype),
        compiler_params=pltpu.CompilerParams(vmem_limit_bytes=VMEM_MIB * 1024 * 1024),
        cost_estimate=pl.CostEstimate(flops=int(1e9), bytes_accessed=4 * rows * n * width, transcendentals=0),
        name="stage",
    )(*[pltpu.with_memory_space_constraint(a, pltpu.HBM) for a in parts], *after)


def project(place, sources, weights, first, width, kind, after=()):
    pair = len(weights)
    tokens = sources[0].shape[0]
    rows = weights[0].shape[0]

    def body(ins, outs):
        place, sources, weights = ins[0], ins[1 : 1 + len(sources_in)], ins[1 + len(sources_in) :]
        lhs = []
        for i in range(pair):
            start = (place[0] * pair + (place[1] + i) % pair) * rows
            part = pl.ds(pl.multiple_of(start, rows), rows)
            blocks = [ref[:, part] for ref in sources]
            lhs.append(blocks[0] if len(blocks) == 1 else jnp.concatenate(blocks, axis=0))
        for at in range(0, width, LANES):
            cols = slice(at, at + LANES)
            from_cols = slice(first + at, first + at + LANES)
            total = dot(lhs[0], weights[0][:, from_cols], 1, 0)
            for i in range(1, pair):
                total += dot(lhs[i], weights[i][:, from_cols], 1, 0)
            for j, ref in enumerate(outs):
                ref[:, cols] = total[j * tokens : (j + 1) * tokens].astype(kind)

    sources_in = list(sources)
    return call(
        body, "project", [*sources, *weights], [(tokens, width, kind, True)] * len(sources), after, (place,), (len(sources), len(sources) + 1),
    )


def combine(local, parts, attn_out, lse, first, cuts, size, after=()):
    tokens, width = local.shape
    head0 = first // size

    def body(ins, outs):
        local, parts, attn_out, lse = ins[0], ins[1:-2], ins[-2], ins[-1]
        done = 0
        for msg, heads in zip(outs, cuts):
            here = slice(done * size, (done + heads) * size)
            place = slice(first + here.start, first + here.stop)
            total = local[:, here]
            for ref in parts:
                total += ref[:, here].astype(F32)
            grad = total.astype(BF16)
            msg[:tokens, :] = grad
            product = grad.astype(F32) * attn_out[:, place].astype(F32)
            high = product.astype(BF16)
            low = (product - high.astype(F32)).astype(BF16)
            ones = jnp.ones((8, size), BF16)
            rows, lses = [], []
            for h in range(heads):
                cols = slice(h * size, (h + 1) * size)
                line = slice(head0 + done + h, head0 + done + h + 1)
                rows.append(dot(ones, high[:, cols], 1, 1) + dot(ones, low[:, cols], 1, 1))
                lses.append(jnp.broadcast_to(lse[line, :], (8, tokens)))
            pick = lax.broadcasted_iota(jnp.int32, (8, heads * size), 0)
            both = jnp.where(pick < 3, jnp.concatenate(rows, axis=1), jnp.concatenate(lses, axis=1))
            first_part = both.astype(BF16).astype(F32)
            rest = both - first_part
            second = rest.astype(BF16).astype(F32)
            third = rest - second
            turn = jnp.where(pick < 3, pick, pick - 3)
            kept = jnp.where(turn == 0, first_part, jnp.where(turn == 1, second, third))
            msg[tokens:, :] = jnp.concatenate([kept, kept], axis=0).astype(BF16)
            done += heads

    return call(
        body, "combine", [local, *parts, attn_out, lse],
        [(tokens + EXTRA, heads * size, BF16, True) for heads in cuts], after,
    )


def rows_of(msg, tokens, cols):
    tail = msg[tokens:, cols].astype(F32)
    return tail[0:1] + tail[1:2] + tail[2:3], tail[3:4] + tail[4:5] + tail[5:6]


def bias_of(order, key_block, query_block, tokens):
    def position(block, axis):
        at = lax.broadcasted_iota(jnp.int32, (tokens, tokens), axis)
        count = tokens // GROUP
        base = jnp.full((tokens, tokens), order[block * count] * GROUP, jnp.int32)
        for g in range(1, count):
            base = jnp.where(at >= g * GROUP, (order[block * count + g] - g) * GROUP, base)
        return base + at

    return jnp.where(position(key_block, 0) <= position(query_block, 1), 0.0, -jnp.inf).astype(F32)


def masks(scalars, tokens, after=()):
    def body(ins, outs):
        order, spots = ins
        for out, (key_block, query_block) in zip(outs, ((0, 0), (0, 1), (2, 0))):
            out[...] = bias_of(order, spots[key_block], spots[query_block], tokens)

    return call(body, "masks", [], [(tokens, tokens, F32, True)] * 3, after, scalars)


def weights_of(q, k, v, g, rows, bias):
    delta, lse = rows
    probs = jnp.exp(dot(k, q, 1, 1) * (q.shape[1] ** -0.5) - lse + bias)
    return probs.astype(BF16), (probs * (dot(v, g, 1, 1) - delta)).astype(BF16)


def places(first, heads, size):
    return [(slice(h * size, (h + 1) * size), slice(first + h * size, first + (h + 1) * size)) for h in range(heads)]


def own_pair(query, key, value, bias, msgs, first, size, extra=0, before=(), after=()):
    tokens = query.shape[0]
    width = sum(msg.shape[1] for msg in msgs)
    factor = size ** -0.5

    def body(ins, outs):
        query, key, value, bias = ins[:4]
        msgs_in, pairs = ins[4 : 4 + len(msgs)], ins[4 + len(msgs) :]
        dq, dk, dv = outs
        done = 0
        for msg in msgs_in:
            for cols, _ in places(0, msg.shape[1] // size, size):
                here = slice(done, done + size)
                place = slice(first + done, first + done + size)
                q, k, v, g = query[:, place], key[:, place], value[:, place], msg[:tokens, cols]
                rows = rows_of(msg, tokens, cols)
                probs, dscores = weights_of(q, k, v, g, rows, bias[...])
                dv[:, here] = dot(probs, g, 1, 0)
                dk[:, here] = dot(dscores, q, 1, 0)
                total = dot(dscores, k, 0, 0)
                at = done - (width - extra * size)
                if at >= 0:
                    k_old = pairs[0][:, at : at + size]
                    v_old = pairs[0][:, extra * size + at : extra * size + at + size]
                    _, dscores = weights_of(q, k_old, v_old, g, rows, pairs[1][...])
                    total += dot(dscores, k_old, 0, 0)
                dq[:, here] = total * factor
                done += size

    return call(
        body, "own_pair", [query, key, value, bias, *msgs, *before], [(tokens, width, F32, True)] * 3, after,
    )


def cross_pair(query, key, value, bias, msg, first, heads, size, after=()):
    tokens, width = query.shape[0], heads * size
    factor = size ** -0.5

    def body(ins, outs):
        query, key, value, bias, msg = ins
        dq, probs_out, dscores_out = outs
        for cols, place in places(first, heads, size):
            q, k, v, g = query[:, place], key[:, place], value[:, place], msg[:tokens, cols]
            probs, dscores = weights_of(q, k, v, g, rows_of(msg, tokens, cols), bias[...])
            probs_out[:, cols] = probs
            dscores_out[:, cols] = dscores
            dq[:, cols] = (dot(dscores, k, 0, 0) * factor).astype(BF16)

    return call(
        body, "cross_pair", [query, key, value, bias, msg], [(tokens, width, BF16, True)] * 3, after,
    )


def key_grads(query, key, value, bias, nexts, owns, knowns, plan, after=()):
    tokens, width = query.shape

    def body(ins, outs):
        query, key, value, bias = ins[:4]
        refs = list(ins[4:])
        dk_out, dv_out = outs
        msgs = [refs.pop(0) for _ in nexts]
        sums = [[refs.pop(0) for _ in own] for own in owns]
        pairs = [[refs.pop(0) for _ in known] for known in knowns]
        for (first, part, heads, extra, step, offset), msg, known in zip(plan, msgs, pairs):
            size = part // heads
            factor = size ** -0.5
            dk, dv = sums[step]
            for h, (cols, place) in enumerate(places(first, heads, size)):
                here = slice(offset + cols.start, offset + cols.stop)
                q, g = query[:, place], msg[:tokens, cols]
                if h < heads - extra:
                    probs, dscores = known[0][:, cols], known[1][:, cols]
                else:
                    rows = rows_of(msg, tokens, cols)
                    probs, dscores = weights_of(q, key[:, place], value[:, place], g, rows, bias[...])
                dk_out[:, place] = ((dk[:, here] + dot(dscores, q, 1, 0)) * factor).astype(BF16)
                dv_out[:, place] = (dv[:, here] + dot(probs, g, 1, 0)).astype(BF16)

    flat = [a for group in (*owns, *knowns) for a in group]
    return call(
        body, "key_grads", [query, key, value, bias, *nexts, *flat], [(tokens, width, BF16, False)] * 2, after,
    )


def query_grads(owns, backs, plan, after=()):
    tokens, width = owns[0].shape[0], sum(step[1] for step in plan)

    def body(ins, outs):
        (out,) = outs
        owns_in, backs_in = ins[: len(owns)], list(ins[len(owns) :])
        for first, part, heads, extra, step, offset in plan:
            sent = part - extra * (part // heads)
            own = owns_in[step]
            if sent:
                out[:, first : first + sent] = (own[:, offset : offset + sent] + backs_in.pop(0)[...].astype(F32)).astype(BF16)
            if extra:
                out[:, first + sent : first + part] = own[:, offset + sent : offset + part].astype(BF16)

    (out,) = call(body, "query_grads", [*owns, *backs], [(tokens, width, BF16, False)], after)
    return out


def on_device(queries, keys, values, out_grad, out_proj, attn_out, log_sum, group_order):
    tokens, width = queries.shape[1:]
    heads = log_sum.shape[1]
    size = width // heads
    rows = out_proj.shape[0]
    query, key, value, upstream, output = queries[0], keys[0], values[0], out_grad[0], attn_out[0]
    lse = log_sum[0]
    dp, ctx = lax.axis_size("dp"), lax.axis_size("ctx")
    me, here = lax.axis_index("dp"), lax.axis_index("ctx")
    pair = 2 if dp % 2 == 0 else 1
    chips = dp // pair
    core, chip = me % pair, me // pair

    def along_dp(array, by):
        return lax.ppermute(array, "dp", [(i, (i + by) % dp) for i in range(dp)])

    def along_ctx(array, by):
        return lax.ppermute(array, "ctx", [(i, (i + by) % ctx) for i in range(ctx)])

    def columns_for(there):
        return lax.dynamic_slice_in_dim(upstream, there * (pair * rows), pair * rows, axis=1)

    pieces = [columns_for((chip + j) % chips) for j in range(1, chips)]
    arrived = [along_dp(piece, pair * (j + 1)) for j, piece in enumerate(pieces)]
    at_own = jnp.stack([chip, core]).astype(jnp.int32)
    at_cut = jnp.stack([jnp.zeros_like(core), core]).astype(jnp.int32)
    weights = [stage([out_proj], 0, width, pieces)]
    if pair == 2:
        weights.append(stage([lax.ppermute(out_proj, "dp", [(i, i ^ 1) for i in range(dp)])], 0, width))
    query_sent, _ = lax.optimization_barrier((query, pieces))
    query_next = along_ctx(query_sent, -1)

    order = group_order[0]
    spots = jnp.stack([here, (here + 1) % ctx, (here + ctx - 1) % ctx]).astype(jnp.int32)
    scalars = (order, spots)

    chunks = CHUNKS if heads == sum(sum(cuts) for cuts in CHUNKS) else ((heads,),)
    both = BOTH if chunks is CHUNKS else 0
    plan, steps, done = [], [], 0
    for cuts in chunks:
        steps.append((done * size, sum(cuts) * size, cuts))
        for count in cuts:
            plan.append((done * size, count * size, count, 0, len(steps) - 1, done * size - steps[-1][0]))
            done += count
    plan[-1] = (*plan[-1][:3], both, *plan[-1][4:])

    backs, held = [], []
    for first, part, _ in steps:
        remote = project(at_cut, arrived, weights, first, part, BF16, after=held) if arrived else []
        held = list(remote[:1])
        backs.append([along_dp(remote[j - 1], -pair * j) for j in range(1, chips)])

    extra = plan[-1][3]
    before = []
    if extra:
        before = [along_ctx(stage([key, value], width - extra * size, extra * size, held), 1)]

    bias_own, bias_next, bias_before = masks(scalars, tokens, held)
    msgs = []
    for c, (first, part, cuts) in enumerate(steps):
        waits = [query_next] if c == 0 else msgs[-1]
        (local,) = project(at_own, [upstream], weights, first, part, F32, after=list(waits) + held)
        msgs.append(combine(local, backs[c], output, lse, first, cuts, size, after=before if c else []))
    nexts = [along_ctx(msg, -1) for group in msgs for msg in group]

    crosses, sent, owns = [], [], []
    for c, (first, part, count, extra, step, _) in enumerate(plan):
        cross = ()
        if count > extra:
            waits = sent[-1:] + [own[0] for own in owns[-1:]]
            cross = cross_pair(query_next, key, value, bias_next, nexts[c], first, count - extra, size, after=waits)
            sent.append(cross[0])
        crosses.append(cross[1:])
        if c + 1 == len(plan) or plan[c + 1][4] > step:
            last = c + 1 == len(plan) and extra
            owns.append(
                own_pair(
                    query, key, value, bias_own, msgs[step], steps[step][0], size, extra if last else 0,
                    (*before, bias_before) if last else (), after=sent[-1:],
                )
            )
    returned = [along_ctx(dq, 1) for dq in sent]
    sums = [own[1:] for own in owns]
    key_grad, value_grad = key_grads(query_next, key, value, bias_next, nexts, sums, crosses, plan)
    query_grad = query_grads([own[0] for own in owns], returned, plan)
    shape = (1, tokens, width)
    return query_grad.reshape(shape), key_grad.reshape(shape), value_grad.reshape(shape)


def solution(mesh):
    return jax.shard_map(
        on_device,
        mesh=mesh,
        in_specs=(
            P("dp", "ctx", None),
            P("dp", "ctx", None),
            P("dp", "ctx", None),
            P("dp", "ctx", None),
            P("dp", None),
            P("dp", "ctx", None),
            P("dp", None, "ctx"),
            P("dp", None),
        ),
        out_specs=(P("dp", "ctx", None), P("dp", "ctx", None), P("dp", "ctx", None)),
        check_vma=False,
    )
```

```python
import functools

import jax
import jax.numpy as jnp
from jax import lax
from jax.experimental import pallas as pl
from jax.experimental.pallas import tpu as pltpu
from jax.sharding import PartitionSpec as P

GROUP = 32
CHUNKS = ((8,), (5, 3))
BOTH = 3
LANES = 256
EXTRA = 16
VMEM_MIB = 20
F32 = jnp.float32
BF16 = jnp.bfloat16


def dot(a, b, ca, cb):
    return lax.dot_general(a, b, (((ca,), (cb,)), ((), ())), preferred_element_type=F32)


def here_in(space):
    return pl.BlockSpec(memory_space=space)


def pin(array):
    return pltpu.with_memory_space_constraint(array, pltpu.VMEM)


def call(body, name, ins, outs, after=(), scalars=(), free=(), work=1e9):
    n_in, n_after = len(scalars) + len(ins), len(after)

    def kernel(*refs):
        body(refs[:n_in], refs[n_in + n_after :])

    moved = sum(a.size * a.dtype.itemsize for a in ins) + sum(jnp.dtype(t).itemsize * r * c for r, c, t, _ in outs)
    return pl.pallas_call(
        kernel,
        in_specs=[here_in(pltpu.SMEM)] * len(scalars) + [here_in(pltpu.VMEM)] * len(ins) + [here_in(pl.ANY)] * n_after,
        out_specs=[here_in(pltpu.VMEM)] * len(outs),
        out_shape=[pltpu.VMEM((r, c), t) if kept else jax.ShapeDtypeStruct((r, c), t) for r, c, t, kept in outs],
        compiler_params=pltpu.CompilerParams(vmem_limit_bytes=VMEM_MIB * 1024 * 1024),
        cost_estimate=pl.CostEstimate(flops=int(work), bytes_accessed=int(1 * moved), transcendentals=0),
        name=name,
    )(*scalars, *[a if i in free else pin(a) for i, a in enumerate(ins)], *after)


def stage(parts, first, width, after=()):
    rows, n, n_after = parts[0].shape[0], len(parts), len(after)
    cuts = 4 if rows % 64 == 0 else 1
    height = rows // cuts

    def kernel(*refs):
        out = refs[n + n_after]

        def copy(semaphores):
            moves = []
            for i in range(n):
                for j in range(cuts):
                    lines = pl.ds(j * height, height)
                    source = refs[i].at[lines, pl.ds(first, width)]
                    target = out.at[lines, pl.ds(i * width, width)]
                    moves.append(pltpu.make_async_copy(source, target, semaphores.at[i * cuts + j]))
                    moves[-1].start()
            for move in moves:
                move.wait()

        pl.run_scoped(copy, pltpu.SemaphoreType.DMA((n * cuts,)))

    return pl.pallas_call(
        kernel,
        in_specs=[here_in(pl.ANY)] * (n + n_after),
        out_specs=here_in(pltpu.VMEM),
        out_shape=pltpu.VMEM((rows, n * width), parts[0].dtype),
        compiler_params=pltpu.CompilerParams(vmem_limit_bytes=VMEM_MIB * 1024 * 1024),
        cost_estimate=pl.CostEstimate(flops=int(1e9), bytes_accessed=4 * rows * n * width, transcendentals=0),
        name="stage",
    )(*[pltpu.with_memory_space_constraint(a, pltpu.HBM) for a in parts], *after)


def project(place, sources, weights, first, width, kind, after=()):
    pair = len(weights)
    tokens = sources[0].shape[0]
    rows = weights[0].shape[0]

    def body(ins, outs):
        place, sources, weights = ins[0], ins[1 : 1 + len(sources_in)], ins[1 + len(sources_in) :]
        lhs = []
        for i in range(pair):
            start = (place[0] * pair + (place[1] + i) % pair) * rows
            part = pl.ds(pl.multiple_of(start, rows), rows)
            blocks = [ref[:, part] for ref in sources]
            lhs.append(blocks[0] if len(blocks) == 1 else jnp.concatenate(blocks, axis=0))
        for at in range(0, width, LANES):
            cols = slice(at, at + LANES)
            from_cols = slice(first + at, first + at + LANES)
            total = dot(lhs[0], weights[0][:, from_cols], 1, 0)
            for i in range(1, pair):
                total += dot(lhs[i], weights[i][:, from_cols], 1, 0)
            for j, ref in enumerate(outs):
                ref[:, cols] = total[j * tokens : (j + 1) * tokens].astype(kind)

    sources_in = list(sources)
    return call(
        body, "project", [*sources, *weights], [(tokens, width, kind, True)] * len(sources), after, (place,), (len(sources), len(sources) + 1),
    )


def combine(local, parts, attn_out, lse, first, cuts, size, after=()):
    tokens, width = local.shape
    head0 = first // size

    def body(ins, outs):
        local, parts, attn_out, lse = ins[0], ins[1:-2], ins[-2], ins[-1]
        done = 0
        for msg, heads in zip(outs, cuts):
            here = slice(done * size, (done + heads) * size)
            place = slice(first + here.start, first + here.stop)
            total = local[:, here]
            for ref in parts:
                total += ref[:, here].astype(F32)
            grad = total.astype(BF16)
            msg[:tokens, :] = grad
            product = grad.astype(F32) * attn_out[:, place].astype(F32)
            high = product.astype(BF16)
            low = (product - high.astype(F32)).astype(BF16)
            ones = jnp.ones((8, size), BF16)
            rows, lses = [], []
            for h in range(heads):
                cols = slice(h * size, (h + 1) * size)
                line = slice(head0 + done + h, head0 + done + h + 1)
                rows.append(dot(ones, high[:, cols], 1, 1) + dot(ones, low[:, cols], 1, 1))
                lses.append(jnp.broadcast_to(lse[line, :], (8, tokens)))
            pick = lax.broadcasted_iota(jnp.int32, (8, heads * size), 0)
            both = jnp.where(pick < 3, jnp.concatenate(rows, axis=1), jnp.concatenate(lses, axis=1))
            first_part = both.astype(BF16).astype(F32)
            rest = both - first_part
            second = rest.astype(BF16).astype(F32)
            third = rest - second
            turn = jnp.where(pick < 3, pick, pick - 3)
            kept = jnp.where(turn == 0, first_part, jnp.where(turn == 1, second, third))
            msg[tokens:, :] = jnp.concatenate([kept, kept], axis=0).astype(BF16)
            done += heads

    return call(
        body, "combine", [local, *parts, attn_out, lse],
        [(tokens + EXTRA, heads * size, BF16, True) for heads in cuts], after,
    )


def rows_of(msg, tokens, cols):
    tail = msg[tokens:, cols].astype(F32)
    return tail[0:1] + tail[1:2] + tail[2:3], tail[3:4] + tail[4:5] + tail[5:6]


def bias_of(order, key_block, query_block, tokens):
    def position(block, axis):
        at = lax.broadcasted_iota(jnp.int32, (tokens, tokens), axis)
        count = tokens // GROUP
        base = jnp.full((tokens, tokens), order[block * count] * GROUP, jnp.int32)
        for g in range(1, count):
            base = jnp.where(at >= g * GROUP, (order[block * count + g] - g) * GROUP, base)
        return base + at

    return jnp.where(position(key_block, 0) <= position(query_block, 1), 0.0, -jnp.inf).astype(F32)


def masks(scalars, tokens, after=()):
    def body(ins, outs):
        order, spots = ins
        for out, (key_block, query_block) in zip(outs, ((0, 0), (0, 1), (2, 0))):
            out[...] = bias_of(order, spots[key_block], spots[query_block], tokens)

    return call(body, "masks", [], [(tokens, tokens, F32, True)] * 3, after, scalars)


def weights_of(q, k, v, g, rows, bias):
    delta, lse = rows
    probs = jnp.exp(dot(k, q, 1, 1) * (q.shape[1] ** -0.5) - lse + bias)
    return probs.astype(BF16), (probs * (dot(v, g, 1, 1) - delta)).astype(BF16)


def places(first, heads, size):
    return [(slice(h * size, (h + 1) * size), slice(first + h * size, first + (h + 1) * size)) for h in range(heads)]


def own_pair(query, key, value, bias, msgs, first, size, extra=0, before=(), after=()):
    tokens = query.shape[0]
    width = sum(msg.shape[1] for msg in msgs)
    factor = size ** -0.5

    def body(ins, outs):
        query, key, value, bias = ins[:4]
        msgs_in, pairs = ins[4 : 4 + len(msgs)], ins[4 + len(msgs) :]
        dq, dk, dv = outs
        done = 0
        for msg in msgs_in:
            for cols, _ in places(0, msg.shape[1] // size, size):
                here = slice(done, done + size)
                place = slice(first + done, first + done + size)
                q, k, v, g = query[:, place], key[:, place], value[:, place], msg[:tokens, cols]
                rows = rows_of(msg, tokens, cols)
                probs, dscores = weights_of(q, k, v, g, rows, bias[...])
                dv[:, here] = dot(probs, g, 1, 0)
                dk[:, here] = dot(dscores, q, 1, 0)
                total = dot(dscores, k, 0, 0)
                at = done - (width - extra * size)
                if at >= 0:
                    k_old = pairs[0][:, at : at + size]
                    v_old = pairs[0][:, extra * size + at : extra * size + at + size]
                    _, dscores = weights_of(q, k_old, v_old, g, rows, pairs[1][...])
                    total += dot(dscores, k_old, 0, 0)
                dq[:, here] = total * factor
                done += size

    return call(
        body, "own_pair", [query, key, value, bias, *msgs, *before], [(tokens, width, F32, True)] * 3, after, work=2e9,
    )


def cross_pair(query, key, value, bias, msg, first, heads, size, after=()):
    tokens, width = query.shape[0], heads * size
    factor = size ** -0.5

    def body(ins, outs):
        query, key, value, bias, msg = ins
        dq, probs_out, dscores_out = outs
        for cols, place in places(first, heads, size):
            q, k, v, g = query[:, place], key[:, place], value[:, place], msg[:tokens, cols]
            probs, dscores = weights_of(q, k, v, g, rows_of(msg, tokens, cols), bias[...])
            probs_out[:, cols] = probs
            dscores_out[:, cols] = dscores
            dq[:, cols] = (dot(dscores, k, 0, 0) * factor).astype(BF16)

    return call(
        body, "cross_pair", [query, key, value, bias, msg], [(tokens, width, BF16, True)] * 3, after,
    )


def key_grads(query, key, value, bias, nexts, owns, knowns, plan, after=()):
    tokens, width = query.shape

    def body(ins, outs):
        query, key, value, bias = ins[:4]
        refs = list(ins[4:])
        dk_out, dv_out = outs
        msgs = [refs.pop(0) for _ in nexts]
        sums = [[refs.pop(0) for _ in own] for own in owns]
        pairs = [[refs.pop(0) for _ in known] for known in knowns]
        for (first, part, heads, extra, step, offset), msg, known in zip(plan, msgs, pairs):
            size = part // heads
            factor = size ** -0.5
            dk, dv = sums[step]
            for h, (cols, place) in enumerate(places(first, heads, size)):
                here = slice(offset + cols.start, offset + cols.stop)
                q, g = query[:, place], msg[:tokens, cols]
                if h < heads - extra:
                    probs, dscores = known[0][:, cols], known[1][:, cols]
                else:
                    rows = rows_of(msg, tokens, cols)
                    probs, dscores = weights_of(q, key[:, place], value[:, place], g, rows, bias[...])
                dk_out[:, place] = ((dk[:, here] + dot(dscores, q, 1, 0)) * factor).astype(BF16)
                dv_out[:, place] = (dv[:, here] + dot(probs, g, 1, 0)).astype(BF16)

    flat = [a for group in (*owns, *knowns) for a in group]
    return call(
        body, "key_grads", [query, key, value, bias, *nexts, *flat], [(tokens, width, BF16, False)] * 2, after, work=2e9,
    )


def query_grads(owns, backs, plan, after=()):
    tokens, width = owns[0].shape[0], sum(step[1] for step in plan)

    def body(ins, outs):
        (out,) = outs
        owns_in, backs_in = ins[: len(owns)], list(ins[len(owns) :])
        for first, part, heads, extra, step, offset in plan:
            sent = part - extra * (part // heads)
            own = owns_in[step]
            if sent:
                out[:, first : first + sent] = (own[:, offset : offset + sent] + backs_in.pop(0)[...].astype(F32)).astype(BF16)
            if extra:
                out[:, first + sent : first + part] = own[:, offset + sent : offset + part].astype(BF16)

    (out,) = call(body, "query_grads", [*owns, *backs], [(tokens, width, BF16, False)], after)
    return out


def on_device(queries, keys, values, out_grad, out_proj, attn_out, log_sum, group_order):
    tokens, width = queries.shape[1:]
    heads = log_sum.shape[1]
    size = width // heads
    rows = out_proj.shape[0]
    query, key, value, upstream, output = queries[0], keys[0], values[0], out_grad[0], attn_out[0]
    lse = log_sum[0]
    dp, ctx = lax.axis_size("dp"), lax.axis_size("ctx")
    me, here = lax.axis_index("dp"), lax.axis_index("ctx")
    pair = 2 if dp % 2 == 0 else 1
    chips = dp // pair
    core, chip = me % pair, me // pair

    def along_dp(array, by):
        return lax.ppermute(array, "dp", [(i, (i + by) % dp) for i in range(dp)])

    def along_ctx(array, by):
        return lax.ppermute(array, "ctx", [(i, (i + by) % ctx) for i in range(ctx)])

    def columns_for(there):
        return lax.dynamic_slice_in_dim(upstream, there * (pair * rows), pair * rows, axis=1)

    pieces = [columns_for((chip + j) % chips) for j in range(1, chips)]
    arrived = [along_dp(piece, pair * (j + 1)) for j, piece in enumerate(pieces)]
    at_own = jnp.stack([chip, core]).astype(jnp.int32)
    at_cut = jnp.stack([jnp.zeros_like(core), core]).astype(jnp.int32)
    weights = [stage([out_proj], 0, width, pieces)]
    if pair == 2:
        weights.append(stage([lax.ppermute(out_proj, "dp", [(i, i ^ 1) for i in range(dp)])], 0, width))
    query_sent, _ = lax.optimization_barrier((query, pieces))
    query_next = along_ctx(query_sent, -1)

    order = group_order[0]
    spots = jnp.stack([here, (here + 1) % ctx, (here + ctx - 1) % ctx]).astype(jnp.int32)
    scalars = (order, spots)

    chunks = CHUNKS if heads == sum(sum(cuts) for cuts in CHUNKS) else ((heads,),)
    both = BOTH if chunks is CHUNKS else 0
    plan, steps, done = [], [], 0
    for cuts in chunks:
        steps.append((done * size, sum(cuts) * size, cuts))
        for count in cuts:
            plan.append((done * size, count * size, count, 0, len(steps) - 1, done * size - steps[-1][0]))
            done += count
    plan[-1] = (*plan[-1][:3], both, *plan[-1][4:])

    backs, held = [], []
    for first, part, _ in steps:
        remote = project(at_cut, arrived, weights, first, part, BF16, after=held) if arrived else []
        held = list(remote[:1])
        backs.append([along_dp(remote[j - 1], -pair * j) for j in range(1, chips)])

    extra = plan[-1][3]
    before = []
    if extra:
        before = [along_ctx(stage([key, value], width - extra * size, extra * size, held), 1)]

    bias_own, bias_next, bias_before = masks(scalars, tokens, held)
    msgs = []
    for c, (first, part, cuts) in enumerate(steps):
        waits = [query_next] if c == 0 else msgs[-1]
        (local,) = project(at_own, [upstream], weights, first, part, F32, after=list(waits) + held)
        msgs.append(combine(local, backs[c], output, lse, first, cuts, size))
    nexts = [along_ctx(msg, -1) for group in msgs for msg in group]

    crosses, sent, owns = [], [], []
    for c, (first, part, count, extra, step, _) in enumerate(plan):
        cross = ()
        if count > extra:
            waits = sent[-1:] + [own[0] for own in owns[-1:]]
            cross = cross_pair(query_next, key, value, bias_next, nexts[c], first, count - extra, size, after=waits)
            sent.append(cross[0])
        crosses.append(cross[1:])
        if c + 1 == len(plan) or plan[c + 1][4] > step:
            last = c + 1 == len(plan) and extra
            owns.append(
                own_pair(
                    query, key, value, bias_own, msgs[step], steps[step][0], size, extra if last else 0,
                    (*before, bias_before) if last else (), after=sent[-1:],
                )
            )
    returned = [along_ctx(dq, 1) for dq in sent]
    sums = [own[1:] for own in owns]
    key_grad, value_grad = key_grads(query_next, key, value, bias_next, nexts, sums, crosses, plan)
    query_grad = query_grads([own[0] for own in owns], returned, plan)
    shape = (1, tokens, width)
    return query_grad.reshape(shape), key_grad.reshape(shape), value_grad.reshape(shape)


def solution(mesh):
    return jax.shard_map(
        on_device,
        mesh=mesh,
        in_specs=(
            P("dp", "ctx", None),
            P("dp", "ctx", None),
            P("dp", "ctx", None),
            P("dp", "ctx", None),
            P("dp", None),
            P("dp", "ctx", None),
            P("dp", None, "ctx"),
            P("dp", None),
        ),
        out_specs=(P("dp", "ctx", None), P("dp", "ctx", None), P("dp", "ctx", None)),
        check_vma=False,
    )
```

```python
import functools

import jax
import jax.numpy as jnp
from jax import lax
from jax.experimental import pallas as pl
from jax.experimental.pallas import tpu as pltpu
from jax.sharding import PartitionSpec as P

GROUP = 32
CHUNKS = ((8,), (5, 3))
BOTH = 3
LANES = 256
EXTRA = 16
VMEM_MIB = 20
F32 = jnp.float32
BF16 = jnp.bfloat16


def dot(a, b, ca, cb):
    return lax.dot_general(a, b, (((ca,), (cb,)), ((), ())), preferred_element_type=F32)


def here_in(space):
    return pl.BlockSpec(memory_space=space)


def pin(array):
    return pltpu.with_memory_space_constraint(array, pltpu.VMEM)


def call(body, name, ins, outs, after=(), scalars=(), free=()):
    n_in, n_after = len(scalars) + len(ins), len(after)

    def kernel(*refs):
        body(refs[:n_in], refs[n_in + n_after :])

    moved = sum(a.size * a.dtype.itemsize for a in ins) + sum(jnp.dtype(t).itemsize * r * c for r, c, t, _ in outs)
    return pl.pallas_call(
        kernel,
        in_specs=[here_in(pltpu.SMEM)] * len(scalars) + [here_in(pltpu.VMEM)] * len(ins) + [here_in(pl.ANY)] * n_after,
        out_specs=[here_in(pltpu.VMEM)] * len(outs),
        out_shape=[pltpu.VMEM((r, c), t) if kept else jax.ShapeDtypeStruct((r, c), t) for r, c, t, kept in outs],
        compiler_params=pltpu.CompilerParams(vmem_limit_bytes=VMEM_MIB * 1024 * 1024),
        cost_estimate=pl.CostEstimate(flops=int(1e9), bytes_accessed=int(1 * moved), transcendentals=0),
        name=name,
    )(*scalars, *[a if i in free else pin(a) for i, a in enumerate(ins)], *after)


def stage(parts, first, width, after=()):
    rows, n, n_after = parts[0].shape[0], len(parts), len(after)
    cuts = 4 if rows % 64 == 0 else 1
    height = rows // cuts

    def kernel(*refs):
        out = refs[n + n_after]

        def copy(semaphores):
            moves = []
            for i in range(n):
                for j in range(cuts):
                    lines = pl.ds(j * height, height)
                    source = refs[i].at[lines, pl.ds(first, width)]
                    target = out.at[lines, pl.ds(i * width, width)]
                    moves.append(pltpu.make_async_copy(source, target, semaphores.at[i * cuts + j]))
                    moves[-1].start()
            for move in moves:
                move.wait()

        pl.run_scoped(copy, pltpu.SemaphoreType.DMA((n * cuts,)))

    return pl.pallas_call(
        kernel,
        in_specs=[here_in(pl.ANY)] * (n + n_after),
        out_specs=here_in(pltpu.VMEM),
        out_shape=pltpu.VMEM((rows, n * width), parts[0].dtype),
        compiler_params=pltpu.CompilerParams(vmem_limit_bytes=VMEM_MIB * 1024 * 1024),
        cost_estimate=pl.CostEstimate(flops=int(1e9), bytes_accessed=4 * rows * n * width, transcendentals=0),
        name="stage",
    )(*[pltpu.with_memory_space_constraint(a, pltpu.HBM) for a in parts], *after)


def project(place, sources, weights, first, width, kind, after=()):
    pair = len(weights)
    tokens = sources[0].shape[0]
    rows = weights[0].shape[0]

    def body(ins, outs):
        place, sources, weights = ins[0], ins[1 : 1 + len(sources_in)], ins[1 + len(sources_in) :]
        lhs = []
        for i in range(pair):
            start = (place[0] * pair + (place[1] + i) % pair) * rows
            part = pl.ds(pl.multiple_of(start, rows), rows)
            blocks = [ref[:, part] for ref in sources]
            lhs.append(blocks[0] if len(blocks) == 1 else jnp.concatenate(blocks, axis=0))
        for at in range(0, width, LANES):
            cols = slice(at, at + LANES)
            from_cols = slice(first + at, first + at + LANES)
            total = dot(lhs[0], weights[0][:, from_cols], 1, 0)
            for i in range(1, pair):
                total += dot(lhs[i], weights[i][:, from_cols], 1, 0)
            for j, ref in enumerate(outs):
                ref[:, cols] = total[j * tokens : (j + 1) * tokens].astype(kind)

    sources_in = list(sources)
    return call(
        body, "project", [*sources, *weights], [(tokens, width, kind, True)] * len(sources), after, (place,), (len(sources), len(sources) + 1),
    )


def combine(local, parts, attn_out, lse, first, cuts, size, after=()):
    tokens, width = local.shape
    head0 = first // size

    def body(ins, outs):
        local, parts, attn_out, lse = ins[0], ins[1:-2], ins[-2], ins[-1]
        done = 0
        for msg, heads in zip(outs, cuts):
            here = slice(done * size, (done + heads) * size)
            place = slice(first + here.start, first + here.stop)
            total = local[:, here]
            for ref in parts:
                total += ref[:, here].astype(F32)
            grad = total.astype(BF16)
            msg[:tokens, :] = grad
            product = grad.astype(F32) * attn_out[:, place].astype(F32)
            high = product.astype(BF16)
            low = (product - high.astype(F32)).astype(BF16)
            ones = jnp.ones((8, size), BF16)
            rows, lses = [], []
            for h in range(heads):
                cols = slice(h * size, (h + 1) * size)
                line = slice(head0 + done + h, head0 + done + h + 1)
                rows.append(dot(ones, high[:, cols], 1, 1) + dot(ones, low[:, cols], 1, 1))
                lses.append(jnp.broadcast_to(lse[line, :], (8, tokens)))
            pick = lax.broadcasted_iota(jnp.int32, (8, heads * size), 0)
            both = jnp.where(pick < 3, jnp.concatenate(rows, axis=1), jnp.concatenate(lses, axis=1))
            first_part = both.astype(BF16).astype(F32)
            rest = both - first_part
            second = rest.astype(BF16).astype(F32)
            third = rest - second
            turn = jnp.where(pick < 3, pick, pick - 3)
            kept = jnp.where(turn == 0, first_part, jnp.where(turn == 1, second, third))
            msg[tokens:, :] = jnp.concatenate([kept, kept], axis=0).astype(BF16)
            done += heads

    return call(
        body, "combine", [local, *parts, attn_out, lse],
        [(tokens + EXTRA, heads * size, BF16, True) for heads in cuts], after,
    )


def rows_of(msg, tokens, cols):
    tail = msg[tokens:, cols].astype(F32)
    return tail[0:1] + tail[1:2] + tail[2:3], tail[3:4] + tail[4:5] + tail[5:6]


def bias_of(order, key_block, query_block, tokens):
    def position(block, axis):
        at = lax.broadcasted_iota(jnp.int32, (tokens, tokens), axis)
        count = tokens // GROUP
        base = jnp.full((tokens, tokens), order[block * count] * GROUP, jnp.int32)
        for g in range(1, count):
            base = jnp.where(at >= g * GROUP, (order[block * count + g] - g) * GROUP, base)
        return base + at

    return jnp.where(position(key_block, 0) <= position(query_block, 1), 0.0, -jnp.inf).astype(F32)


def masks(scalars, tokens, after=()):
    def body(ins, outs):
        order, spots = ins
        for out, (key_block, query_block) in zip(outs, ((0, 0), (0, 1), (2, 0))):
            out[...] = bias_of(order, spots[key_block], spots[query_block], tokens)

    return call(body, "masks", [], [(tokens, tokens, F32, True)] * 3, after, scalars)


def weights_of(q, k, v, g, rows, bias):
    delta, lse = rows
    probs = jnp.exp(dot(k, q, 1, 1) * (q.shape[1] ** -0.5) - lse + bias)
    return probs.astype(BF16), (probs * (dot(v, g, 1, 1) - delta)).astype(BF16)


def places(first, heads, size):
    return [(slice(h * size, (h + 1) * size), slice(first + h * size, first + (h + 1) * size)) for h in range(heads)]


def own_pair(query, key, value, bias, msgs, first, size, extra=0, before=(), after=()):
    tokens = query.shape[0]
    width = sum(msg.shape[1] for msg in msgs)
    factor = size ** -0.5

    def body(ins, outs):
        query, key, value, bias = ins[:4]
        msgs_in, pairs = ins[4 : 4 + len(msgs)], ins[4 + len(msgs) :]
        dq, dk, dv = outs
        done = 0
        for msg in msgs_in:
            for cols, _ in places(0, msg.shape[1] // size, size):
                here = slice(done, done + size)
                place = slice(first + done, first + done + size)
                q, k, v, g = query[:, place], key[:, place], value[:, place], msg[:tokens, cols]
                rows = rows_of(msg, tokens, cols)
                probs, dscores = weights_of(q, k, v, g, rows, bias[...])
                dv[:, here] = dot(probs, g, 1, 0)
                dk[:, here] = dot(dscores, q, 1, 0)
                total = dot(dscores, k, 0, 0)
                at = done - (width - extra * size)
                if at >= 0:
                    k_old = pairs[0][:, at : at + size]
                    v_old = pairs[0][:, extra * size + at : extra * size + at + size]
                    _, dscores = weights_of(q, k_old, v_old, g, rows, pairs[1][...])
                    total += dot(dscores, k_old, 0, 0)
                dq[:, here] = total * factor
                done += size

    return call(
        body, "own_pair", [query, key, value, bias, *msgs, *before], [(tokens, width, F32, True)] * 3, after,
    )


def cross_pair(query, key, value, bias, msg, first, heads, size, after=()):
    tokens, width = query.shape[0], heads * size
    factor = size ** -0.5

    def body(ins, outs):
        query, key, value, bias, msg = ins
        dq, probs_out, dscores_out = outs
        for cols, place in places(first, heads, size):
            q, k, v, g = query[:, place], key[:, place], value[:, place], msg[:tokens, cols]
            probs, dscores = weights_of(q, k, v, g, rows_of(msg, tokens, cols), bias[...])
            probs_out[:, cols] = probs
            dscores_out[:, cols] = dscores
            dq[:, cols] = (dot(dscores, k, 0, 0) * factor).astype(BF16)

    return call(
        body, "cross_pair", [query, key, value, bias, msg], [(tokens, width, BF16, True)] * 3, after,
    )


def key_grads(query, key, value, bias, nexts, owns, knowns, plan, after=()):
    tokens, width = query.shape

    def body(ins, outs):
        query, key, value, bias = ins[:4]
        refs = list(ins[4:])
        dk_out, dv_out = outs
        msgs = [refs.pop(0) for _ in nexts]
        sums = [[refs.pop(0) for _ in own] for own in owns]
        pairs = [[refs.pop(0) for _ in known] for known in knowns]
        for (first, part, heads, extra, step, offset), msg, known in zip(plan, msgs, pairs):
            size = part // heads
            factor = size ** -0.5
            dk, dv = sums[step]
            for h, (cols, place) in enumerate(places(first, heads, size)):
                here = slice(offset + cols.start, offset + cols.stop)
                q, g = query[:, place], msg[:tokens, cols]
                if h < heads - extra:
                    probs, dscores = known[0][:, cols], known[1][:, cols]
                else:
                    rows = rows_of(msg, tokens, cols)
                    probs, dscores = weights_of(q, key[:, place], value[:, place], g, rows, bias[...])
                dk_out[:, place] = ((dk[:, here] + dot(dscores, q, 1, 0)) * factor).astype(BF16)
                dv_out[:, place] = (dv[:, here] + dot(probs, g, 1, 0)).astype(BF16)

    flat = [a for group in (*owns, *knowns) for a in group]
    return call(
        body, "key_grads", [query, key, value, bias, *nexts, *flat], [(tokens, width, BF16, False)] * 2, after,
    )


def query_grads(owns, backs, plan, after=()):
    tokens, width = owns[0].shape[0], sum(step[1] for step in plan)

    def body(ins, outs):
        (out,) = outs
        owns_in, backs_in = ins[: len(owns)], list(ins[len(owns) :])
        for first, part, heads, extra, step, offset in plan:
            sent = part - extra * (part // heads)
            own = owns_in[step]
            if sent:
                out[:, first : first + sent] = (own[:, offset : offset + sent] + backs_in.pop(0)[...].astype(F32)).astype(BF16)
            if extra:
                out[:, first + sent : first + part] = own[:, offset + sent : offset + part].astype(BF16)

    (out,) = call(body, "query_grads", [*owns, *backs], [(tokens, width, BF16, False)], after)
    return out


def on_device(queries, keys, values, out_grad, out_proj, attn_out, log_sum, group_order):
    tokens, width = queries.shape[1:]
    heads = log_sum.shape[1]
    size = width // heads
    rows = out_proj.shape[0]
    query, key, value, upstream, output = queries[0], keys[0], values[0], out_grad[0], attn_out[0]
    lse = log_sum[0]
    dp, ctx = lax.axis_size("dp"), lax.axis_size("ctx")
    me, here = lax.axis_index("dp"), lax.axis_index("ctx")
    pair = 2 if dp % 2 == 0 else 1
    chips = dp // pair
    core, chip = me % pair, me // pair

    def along_dp(array, by):
        return lax.ppermute(array, "dp", [(i, (i + by) % dp) for i in range(dp)])

    def along_ctx(array, by):
        return lax.ppermute(array, "ctx", [(i, (i + by) % ctx) for i in range(ctx)])

    def columns_for(there):
        return lax.dynamic_slice_in_dim(upstream, there * (pair * rows), pair * rows, axis=1)

    pieces = [columns_for((chip + j) % chips) for j in range(1, chips)]
    arrived = [along_dp(piece, pair * (j + 1)) for j, piece in enumerate(pieces)]
    at_own = jnp.stack([chip, core]).astype(jnp.int32)
    at_cut = jnp.stack([jnp.zeros_like(core), core]).astype(jnp.int32)
    weights = [stage([out_proj], 0, width, pieces)]
    if pair == 2:
        weights.append(stage([lax.ppermute(lax.optimization_barrier((out_proj, pieces))[0], "dp", [(i, i ^ 1) for i in range(dp)])], 0, width))
    query_sent, _ = lax.optimization_barrier((query, pieces))
    query_next = along_ctx(query_sent, -1)

    order = group_order[0]
    spots = jnp.stack([here, (here + 1) % ctx, (here + ctx - 1) % ctx]).astype(jnp.int32)
    scalars = (order, spots)

    chunks = CHUNKS if heads == sum(sum(cuts) for cuts in CHUNKS) else ((heads,),)
    both = BOTH if chunks is CHUNKS else 0
    plan, steps, done = [], [], 0
    for cuts in chunks:
        steps.append((done * size, sum(cuts) * size, cuts))
        for count in cuts:
            plan.append((done * size, count * size, count, 0, len(steps) - 1, done * size - steps[-1][0]))
            done += count
    plan[-1] = (*plan[-1][:3], both, *plan[-1][4:])

    backs, held = [], []
    for first, part, _ in steps:
        remote = project(at_cut, arrived, weights, first, part, BF16, after=held) if arrived else []
        held = list(remote[:1])
        backs.append([along_dp(remote[j - 1], -pair * j) for j in range(1, chips)])

    extra = plan[-1][3]
    before = []
    if extra:
        before = [along_ctx(stage([key, value], width - extra * size, extra * size, held), 1)]

    bias_own, bias_next, bias_before = masks(scalars, tokens, held)
    msgs = []
    for c, (first, part, cuts) in enumerate(steps):
        waits = [query_next] if c == 0 else msgs[-1]
        (local,) = project(at_own, [upstream], weights, first, part, F32, after=list(waits) + held)
        msgs.append(combine(local, backs[c], output, lse, first, cuts, size, after=before if c else []))
    nexts = [along_ctx(msg, -1) for group in msgs for msg in group]

    crosses, sent, owns = [], [], []
    for c, (first, part, count, extra, step, _) in enumerate(plan):
        cross = ()
        if count > extra:
            waits = sent[-1:] + [own[0] for own in owns[-1:]]
            cross = cross_pair(query_next, key, value, bias_next, nexts[c], first, count - extra, size, after=waits)
            sent.append(cross[0])
        crosses.append(cross[1:])
        if c + 1 == len(plan) or plan[c + 1][4] > step:
            last = c + 1 == len(plan) and extra
            owns.append(
                own_pair(
                    query, key, value, bias_own, msgs[step], steps[step][0], size, extra if last else 0,
                    (*before, bias_before) if last else (), after=sent[-1:],
                )
            )
    returned = [along_ctx(dq, 1) for dq in sent]
    sums = [own[1:] for own in owns]
    key_grad, value_grad = key_grads(query_next, key, value, bias_next, nexts, sums, crosses, plan)
    query_grad = query_grads([own[0] for own in owns], returned, plan)
    shape = (1, tokens, width)
    return query_grad.reshape(shape), key_grad.reshape(shape), value_grad.reshape(shape)


def solution(mesh):
    return jax.shard_map(
        on_device,
        mesh=mesh,
        in_specs=(
            P("dp", "ctx", None),
            P("dp", "ctx", None),
            P("dp", "ctx", None),
            P("dp", "ctx", None),
            P("dp", None),
            P("dp", "ctx", None),
            P("dp", None, "ctx"),
            P("dp", None),
        ),
        out_specs=(P("dp", "ctx", None), P("dp", "ctx", None), P("dp", "ctx", None)),
        check_vma=False,
    )
```
